128 devices in a mesh: grid: 16 (over y, x), mesh: 8 (over z, core).
Axes of the slice: x: 4, y: 4, z: 4, core: 2. Of those that a mesh axis runs over, the one named last changes fastest.
Arguments:
- grid_latent: bfloat16 [65536, 512], P(('grid', 'mesh')), may hold values from -6 to 6
- mesh_latent: bfloat16 [40960, 512], P(('grid', 'mesh')), may hold values from -6 to 6
- edge_latent: bfloat16 [128, 8, 256, 512], P(('grid', 'mesh')), may hold values from -6 to 6
- edge_sender: int32 [128, 8, 256], P(('grid', 'mesh')), may hold values from 0 to 511
- edge_receiver: int32 [128, 8, 256], P(('grid', 'mesh')), may hold values from 0 to 319
- edge_count: int32 [128, 8], P(('grid', 'mesh')), may hold values from 1 to 256, as said below
- edge_in_weight: bfloat16 [1536, 512], replicated, may hold values from -0.15625 to 0.15625
- edge_bias: bfloat16 [512], replicated, may hold values from -3 to 3
- edge_out_weight: bfloat16 [512, 512], replicated, may hold values from -0.25 to 0.25
- edge_gain: bfloat16 [512], replicated, may hold values from 0.25 to 1.75
- node_in_weight: bfloat16 [1024, 512], replicated, may hold values from -0.1875 to 0.1875
- node_bias: bfloat16 [512], replicated, may hold values from -3 to 3
- node_out_weight: bfloat16 [512, 512], replicated, may hold values from -0.25 to 0.25
- node_gain: bfloat16 [512], replicated, may hold values from 0.25 to 1.75
- grid_in_weight: bfloat16 [512, 512], replicated, may hold values from -0.25 to 0.25
- grid_bias: bfloat16 [512], replicated, may hold values from -3 to 3
- grid_out_weight: bfloat16 [512, 512], replicated, may hold values from -0.25 to 0.25
- grid_gain: bfloat16 [512], replicated, may hold values from 0.25 to 1.75
- mesh_cotangent: bfloat16 [40960, 512], P(('grid', 'mesh')), may hold values from -6 to 6
- grid_cotangent: bfloat16 [65536, 512], P(('grid', 'mesh')), may hold values from -6 to 6
Outputs:
- mesh_updated: bfloat16 [40960, 512], P(('grid', 'mesh'))
- grid_updated: bfloat16 [65536, 512], P(('grid', 'mesh'))
- grad_grid: bfloat16 [65536, 512], P(('grid', 'mesh'))
- grad_mesh: bfloat16 [40960, 512], P(('grid', 'mesh'))
- grad_edge: bfloat16 [128, 8, 256, 512], P(('grid', 'mesh'))
The draws below stay inside these ranges and needn't reach their ends.
Inputs may be any that keep to these rules, and one draw needn't show every extreme that they name: `edge_count`: in each row p, at least one of the 8 blocks is full, at a position drawn from the seed.
All inputs are finite; a program needn't handle non-finite values.
Results may differ from the reference program's by a relative error of at most 0.02.
Values may be sent and summed in bfloat16 or wider, within the bound.
A program may use at most 128 MiB of HBM per device.

```python
import jax
import jax.numpy as jnp
from jax import lax

D = 512
BAND = 8
GRID_DEV = 512
MESH_DEV = 320
SLOT_DEV = 2048
CAP = 256
GRID = 65536
MESH = 40960
DEVICES = 128


def draw_edge_count(key, part):
    key = jax.random.fold_in(key, 11)
    first_key, second_key = jax.random.split(key)
    counts = jax.random.randint(first_key, (DEVICES, BAND), 1, CAP + 1, dtype=jnp.int32)
    full_column = jax.random.randint(second_key, (DEVICES, 1), 0, BAND, dtype=jnp.int32)
    column_index = jnp.arange(BAND, dtype=jnp.int32)[None, :]
    return jnp.where(column_index == full_column, jnp.int32(CAP), counts).astype(jnp.int32)


def set_ends(result, own_key, least, high):
    extent = result.shape
    index_at = [jax.random.randint(jax.random.fold_in(own_key, axis), (), 0, extent[axis]) for axis in range(len(extent))]
    result = result.at[tuple(index_at)].set(least)
    longest = extent.index(max(extent))
    index_at[longest] = (index_at[longest] + 1) % extent[longest]
    return result.at[tuple(index_at)].set(high)


def level_of(stream_key, shape, cuts, least, largest):
    level = 1.0
    for dim, shards_of in cuts:
        draws = jax.random.uniform(jax.random.fold_in(jax.random.fold_in(stream_key, 6), dim), (shards_of,), jnp.float32, least / len(cuts), largest / len(cuts))
        level = level * jnp.repeat(jnp.exp(draws), shape[dim] // shards_of).reshape((-1,) + (1,) * (len(shape) - 1 - dim))
    return level


def gaussian(rng, extent, scale, reach, cuts=(), kind=jnp.bfloat16):
    level = level_of(rng, extent, cuts, -0.22, 0.18) if cuts else 1.0
    array = jax.random.normal(rng, extent, jnp.float32) * scale * level
    return jnp.minimum(jnp.maximum(array, -reach), reach).astype(kind)


def setup_inputs(seed: int = 0) -> dict:
    arg_keys = jax.random.split(jax.random.key(seed), 21)
    return {
        "grid_latent": gaussian(arg_keys[0], (GRID, D), 1.0, 6.0, ((0, 128),)),
        "mesh_latent": gaussian(arg_keys[1], (MESH, D), 1.0, 6.0, ((0, 128),)),
        "edge_latent": gaussian(arg_keys[2], (DEVICES, BAND, CAP, D), 1.0, 6.0, ((0, 128),)),
        "edge_sender": set_ends(jax.random.randint(arg_keys[3], (DEVICES, BAND, CAP), 0, GRID_DEV), jax.random.fold_in(arg_keys[3], 1), 0, GRID_DEV - 1).astype(jnp.int32),
        "edge_receiver": set_ends(jax.random.randint(arg_keys[4], (DEVICES, BAND, CAP), 0, MESH_DEV), jax.random.fold_in(arg_keys[4], 1), 0, MESH_DEV - 1).astype(jnp.int32),
        "edge_count": draw_edge_count(jax.random.fold_in(arg_keys[20], 71), 0),
        "edge_in_weight": gaussian(arg_keys[6], (3 * D, D), (3 * D) ** -0.5, 0.15625),
        "edge_bias": gaussian(arg_keys[7], (D,), 0.5, 3.0),
        "edge_out_weight": gaussian(arg_keys[8], (D, D), D ** -0.5, 0.25),
        "edge_gain": jnp.clip(1.0 + 0.15 * jax.random.normal(arg_keys[9], (D,), jnp.float32), 0.25, 1.75).astype(jnp.bfloat16),
        "node_in_weight": gaussian(arg_keys[10], (2 * D, D), (2 * D) ** -0.5, 0.1875),
        "node_bias": gaussian(arg_keys[11], (D,), 0.5, 3.0),
        "node_out_weight": gaussian(arg_keys[12], (D, D), D ** -0.5, 0.25),
        "node_gain": jnp.clip(1.0 + 0.15 * jax.random.normal(arg_keys[13], (D,), jnp.float32), 0.25, 1.75).astype(jnp.bfloat16),
        "grid_in_weight": gaussian(arg_keys[14], (D, D), D ** -0.5, 0.25),
        "grid_bias": gaussian(arg_keys[15], (D,), 0.5, 3.0),
        "grid_out_weight": gaussian(arg_keys[16], (D, D), D ** -0.5, 0.25),
        "grid_gain": jnp.clip(1.0 + 0.15 * jax.random.normal(arg_keys[17], (D,), jnp.float32), 0.25, 1.75).astype(jnp.bfloat16),
        "mesh_cotangent": gaussian(arg_keys[18], (MESH, D), 1.0, 6.0, ((0, 128),)),
        "grid_cotangent": gaussian(arg_keys[19], (GRID, D), 1.0, 6.0, ((0, 128),)),
    }


def layer_norm(values, gain_row):
    row_mean = lax.optimization_barrier(jnp.mean(values, axis=-1, keepdims=True))
    centred = values - row_mean
    row_var = lax.optimization_barrier(jnp.mean(centred * centred, axis=-1, keepdims=True))
    return gain_row.astype(jnp.float32) * centred * lax.rsqrt(row_var + 1e-05)

def two_layer(joined, weight_in, bias_row, weight_out, gain_row):
    first = jnp.dot(joined, weight_in, preferred_element_type=jnp.float32) + bias_row.astype(jnp.float32)
    hidden = jax.nn.silu(first).astype(jnp.bfloat16)
    return layer_norm(jnp.dot(hidden, weight_out, preferred_element_type=jnp.float32), gain_row)

def reference(grid_latent, mesh_latent, edge_latent, edge_sender, edge_receiver, edge_count, edge_in_weight, edge_bias, edge_out_weight, edge_gain, node_in_weight, node_bias, node_out_weight, node_gain, grid_in_weight, grid_bias, grid_out_weight, grid_gain, mesh_cotangent, grid_cotangent):
    slot_index = jnp.arange(CAP, dtype=jnp.int32)
    block_index = jnp.arange(BAND, dtype=jnp.int32)

    def edge_fn(edge_in, grid_in, mesh_in):
        joined = jnp.concatenate([edge_in, grid_in, mesh_in], axis=-1)
        return edge_in.astype(jnp.float32) + two_layer(joined, edge_in_weight, edge_bias, edge_out_weight, edge_gain)

    def node_fn(mesh_in, aggregate_in):
        joined = jnp.concatenate([mesh_in, aggregate_in], axis=-1)
        return mesh_in.astype(jnp.float32) + two_layer(joined, node_in_weight, node_bias, node_out_weight, node_gain)

    def grid_fn(grid_in):
        return grid_in.astype(jnp.float32) + two_layer(grid_in, grid_in_weight, grid_bias, grid_out_weight, grid_gain)

    def block_inputs(source):
        edge_rows = edge_latent[source].reshape(SLOT_DEV, D)
        local_sender = edge_sender[source].reshape(SLOT_DEV)
        senders = local_sender + source * GRID_DEV
        owners = jnp.mod(source + block_index - BAND // 2, DEVICES).astype(jnp.int32)
        receivers = (edge_receiver[source] + owners[:, None] * MESH_DEV).reshape(SLOT_DEV)
        is_alive = (slot_index[None, :] < edge_count[source][:, None]).reshape(SLOT_DEV)
        return (edge_rows, grid_latent[senders], mesh_latent[receivers], local_sender, receivers, is_alive)

    def forward_step(summed, source):
        edge_rows, grid_rows, mesh_rows, local_sender, receivers, is_alive = block_inputs(source)
        message = edge_fn(edge_rows, grid_rows, mesh_rows).astype(jnp.bfloat16).astype(jnp.float32)
        message = jnp.where(is_alive[:, None], message, jnp.zeros((), jnp.float32))
        return (summed.at[receivers].add(message), None)
    sources = jnp.arange(DEVICES, dtype=jnp.int32)
    summed, _ = lax.scan(forward_step, jnp.zeros((MESH, D), jnp.float32), sources)
    aggregate = summed.astype(jnp.bfloat16)
    node_value, node_backward = jax.vjp(node_fn, mesh_latent, aggregate)
    mesh_updated = node_value.astype(jnp.bfloat16)
    node_grad_mesh, grad_aggregate = node_backward(mesh_cotangent.astype(jnp.float32))

    def backward_step(summed_mesh, source):
        edge_rows, grid_rows, mesh_rows, local_sender, receivers, is_alive = block_inputs(source)
        _, edge_backward = jax.vjp(edge_fn, edge_rows, grid_rows, mesh_rows)
        cotangent = jnp.where(is_alive[:, None], grad_aggregate[receivers].astype(jnp.float32), jnp.zeros((), jnp.float32))
        grad_e, grad_g, grad_m = edge_backward(cotangent)
        grid_part = jnp.zeros((GRID_DEV, D), jnp.float32).at[local_sender].add(jnp.where(is_alive[:, None], grad_g.astype(jnp.float32), jnp.zeros((), jnp.float32)))
        summed_mesh = summed_mesh.at[receivers].add(jnp.where(is_alive[:, None], grad_m.astype(jnp.float32), jnp.zeros((), jnp.float32)))
        return (summed_mesh, (grad_e.reshape(BAND, CAP, D), grid_part))
    mesh_sum, (grad_edge, grid_parts) = lax.scan(backward_step, jnp.zeros((MESH, D), jnp.float32), sources)
    grad_mesh = (node_grad_mesh.astype(jnp.float32) + mesh_sum).astype(jnp.bfloat16)
    grid_value, grid_backward = jax.vjp(grid_fn, grid_latent)
    grid_updated = grid_value.astype(jnp.bfloat16)
    grid_node_grad = grid_backward(grid_cotangent.astype(jnp.float32))[0]
    grad_grid = (grid_node_grad.astype(jnp.float32) + grid_parts.reshape(GRID, D)).astype(jnp.bfloat16)
    return (mesh_updated, grid_updated, grad_grid, grad_mesh, grad_edge)
```

```python
import functools

import jax
import jax.numpy as jnp
from jax import lax
from jax.experimental import pallas as pl
from jax.experimental.pallas import tpu as pltpu
from jax.sharding import PartitionSpec as P

F32 = jnp.float32
BF16 = jnp.bfloat16


def mm(a, b):
    return jnp.dot(a, b, preferred_element_type=F32)


def mm_t(a, b):
    return lax.dot_general(a, b, (((1,), (1,)), ((), ())), preferred_element_type=F32)


def silu_pair(u):
    gate = 0.5 + 0.5 * jnp.tanh(0.5 * u)
    value = u * gate
    return value, gate + value * (1.0 - gate)


def normed(v):
    centred = v - jnp.mean(v, axis=-1, keepdims=True)
    inv = lax.rsqrt(jnp.mean(centred * centred, axis=-1, keepdims=True) + 1e-05)
    return centred * inv, inv


def normed_back(dx, unit, inv):
    along = jnp.mean(dx * unit, axis=-1, keepdims=True)
    return inv * (dx - jnp.mean(dx, axis=-1, keepdims=True) - unit * along)


def kernel(
    sizes,
    grid_hbm,
    mesh_hbm,
    edge_hbm,
    sender,
    receiver,
    count,
    edge_in_hbm,
    edge_out_hbm,
    node_in_hbm,
    node_out_hbm,
    grid_in_hbm,
    grid_out_hbm,
    vectors,
    mesh_cot_hbm,
    grid_cot_hbm,
    mesh_up_hbm,
    grid_up_hbm,
    grad_grid_hbm,
    grad_mesh_hbm,
    grad_edge_hbm,
    grid_v,
    mesh_v,
    edge_v,
    edge_in,
    edge_out,
    node_in,
    node_out,
    grid_in,
    grid_out,
    mesh_cot,
    grid_cot,
    grid_proj,
    recv_row,
    send_col,
    recv_col,
    first_v,
    slope_v,
    unit_v,
    inv_v,
    wanted_v,
    dfirst_v,
    rows_a,
    rows_c,
    part_b,
    pair_b,
    land_b,
    part_d,
    pair_d,
    land_d,
    node_first,
    node_mesh_grad,
    grid_grad,
    mesh_up,
    grid_up,
    grad_grid,
    grad_mesh,
    load_sem,
    out_sem,
    a_send,
    a_recv,
    b_send,
    b_pair,
    b_land,
    c_send,
    c_recv,
    d_send,
    d_pair,
    d_land,
):
    blocks, cap, width, mesh_rows, grid_rows = sizes
    lanes = 128
    fast = lax.axis_size("mesh")
    total = lax.axis_size("grid") * fast
    me = lax.axis_index("grid") * fast + lax.axis_index("mesh")
    core = lax.rem(me, 2)

    def at(shift):
        p = lax.rem(me + (shift + total), total)
        return (lax.div(p, fast), lax.rem(p, fast))

    twin = at(1 - 2 * core)

    def remote(src, dst, send_sem, recv_sem, device):
        return pltpu.make_async_remote_copy(
            src_ref=src,
            dst_ref=dst,
            send_sem=send_sem,
            recv_sem=recv_sem,
            device_id=device,
            device_id_type=pl.DeviceIdType.MESH,
        )

    wide = pl.ds(0, width)
    mid = pl.ds(width, width)
    last = pl.ds(2 * width, width)
    pairs = [
        (mesh_hbm, mesh_v),
        (edge_in_hbm.at[last], edge_in.at[last]),
        (grid_hbm, grid_v),
        (edge_in_hbm.at[mid], edge_in.at[mid]),
        (edge_in_hbm.at[wide], edge_in.at[wide]),
        (edge_hbm.at[0], edge_v),
        (edge_out_hbm, edge_out),
        (node_in_hbm, node_in),
        (node_out_hbm, node_out),
        (mesh_cot_hbm, mesh_cot),
        (grid_in_hbm, grid_in),
        (grid_out_hbm, grid_out),
        (grid_cot_hbm, grid_cot),
    ]
    loads = [pltpu.make_async_copy(src, dst, load_sem.at[i]) for i, (src, dst) in enumerate(pairs)]
    for load in loads:
        load.start()

    barrier = pltpu.get_barrier_semaphore()
    partners = [at(2), at(-2), at(4), at(-4), twin]
    for partner in partners:
        pl.semaphore_signal(
            barrier, inc=1, device_id=partner, device_id_type=pl.DeviceIdType.MESH
        )

    def vector(i):
        return vectors[i : i + 1, :]

    edge_bias, edge_gain, node_bias, node_gain, grid_bias, grid_gain = range(6)

    def spread_copy(i, rows, send, recv):
        routes = [
            (4, 2, at(2)),
            (4, 6, at(-2)),
            (4, 3 + 2 * core, twin),
            (2, 0, at(2)),
            (2, 1 + 2 * core, twin),
            (6, 5 + 2 * core, twin),
            (6, 8, at(-2)),
            (8 - 8 * core, 7 - 6 * core, twin),
        ]
        src, dst, device = routes[i]
        return remote(rows.at[src], rows.at[dst], send.at[i], recv.at[dst], device)

    def spread_arrived(slot, rows, send, recv):
        remote(rows.at[slot], rows.at[slot], send.at[0], recv.at[slot], twin).wait_recv()

    def spread_own(*bufs):
        for i in (0, 1, 2):
            spread_copy(i, *bufs).start()

    def spread_near(*bufs):
        spread_arrived(2, *bufs)
        spread_copy(3, *bufs).start()
        spread_copy(4, *bufs).start()
        spread_arrived(6, *bufs)

        @pl.when(core == 0)
        def _():
            spread_copy(6, *bufs).start()

        spread_copy(5, *bufs).start()

    def spread_far(*bufs):
        spread_arrived(0, *bufs)

        @pl.when(core == 0)
        def _():
            spread_arrived(8, *bufs)

        spread_copy(7, *bufs).start()

    def spread_sent(*bufs):
        for i in (0, 1, 2, 3, 4, 5, 7):
            spread_copy(i, *bufs).wait_send()

        @pl.when(core == 0)
        def _():
            spread_copy(6, *bufs).wait_send()

    def pair_copy(k, part, pair, land, send, pair_sem, land_sem):
        slot = lax.div(k - 1 + 2 * core, 2)
        return remote(part.at[k], pair.at[slot], send.at[k], pair_sem.at[slot], twin)

    def pair_arrived(slot, part, pair, land, send, pair_sem, land_sem):
        remote(pair.at[slot], pair.at[slot], send.at[1], pair_sem.at[slot], twin).wait_recv()

    def land_copy(i, part, pair, land, send, pair_sem, land_sem):
        src, k, device = [
            (part.at[6], 6, at(2)),
            (part.at[2], 2, at(-2)),
            (part.at[0], 0, at(-4)),
            (pair.at[4], 4, at(4)),
        ][i]
        return remote(src, land.at[i], send.at[k], land_sem.at[i], device)

    def join(k, part, pair):
        part[k] = (part[k].astype(F32) + pair[k // 2].astype(F32)).astype(BF16)

    def sum_near(i, *bufs):
        k = (6, 2)[i]
        pair_arrived(k // 2, *bufs)
        join(k, *bufs[:2])
        land_copy(i, *bufs).start()

    def sum_far_first(*bufs):
        @pl.when(core == 0)
        def _():
            land_copy(2, *bufs).start()

    def sum_far_last(*bufs):
        @pl.when(core == 0)
        def _():
            pair_arrived(4, *bufs)
            land_copy(3, *bufs).start()

        @pl.when(core == 1)
        def _():
            pair_arrived(0, *bufs)
            join(0, *bufs[:2])
            land_copy(2, *bufs).start()

    def summed(*bufs):
        part, pair, land = bufs[:3]

        @pl.when(core == 1)
        def _():
            land[3] = jnp.zeros((mesh_rows, width), BF16)

        pair_arrived(2, *bufs)
        for i in (0, 1, 2):
            land_copy(i, *bufs).wait_recv()

        @pl.when(core == 0)
        def _():
            land_copy(3, *bufs).wait_recv()

        value = part[4].astype(F32) + pair[2].astype(F32)
        for i in range(4):
            value = value + land[i].astype(F32)
        return value.astype(BF16)

    def sum_sent(*bufs):
        for k in (1, 3, 5, 7):
            pair_copy(k, *bufs).wait_send()
        for i in (0, 1, 2):
            land_copy(i, *bufs).wait_send()

        @pl.when(core == 0)
        def _():
            land_copy(3, *bufs).wait_send()

    spread_a = (rows_a, a_send, a_recv)
    spread_c = (rows_c, c_send, c_recv)
    sum_b = (part_b, pair_b, land_b, b_send, b_pair, b_land)
    sum_d = (part_d, pair_d, land_d, d_send, d_pair, d_land)

    def pick(column, n):
        tiles = -(-n // lanes)
        ids = jnp.concatenate([column] * tiles, axis=1)[:, :n]
        return jnp.where(lax.broadcasted_iota(jnp.int32, (cap, n), 1) == ids, 1.0, 0.0).astype(BF16)

    def put(row, n, start=0):
        ids = lax.broadcasted_iota(jnp.int32, (n, cap), 0) + start
        return jnp.where(ids == row, 1.0, 0.0).astype(BF16)

    loads[0].wait()
    loads[1].wait()
    rows_a[4] = mm(mesh_v[...], edge_in[last, :]).astype(BF16)
    pl.semaphore_wait(barrier, len(partners))
    spread_own(*spread_a)

    slot_index = lax.broadcasted_iota(jnp.int32, (1, cap), 1)
    for k in range(blocks):
        recv_row[k : k + 1, :] = jnp.where(slot_index < count[0, k], receiver[0, k : k + 1, :], -1)
    for src, dst in ((sender[0], send_col), (recv_row[...], recv_col)):
        turned = jnp.transpose(src)
        for k in range(blocks):
            dst[k] = jnp.broadcast_to(turned[:, k : k + 1], (cap, lanes))

    for load in loads[2:6]:
        load.wait()
    grid_proj[...] = mm(grid_v[...], edge_in[mid, :]).astype(BF16)

    def first_step(k, _):
        first_v[k] = (
            mm(edge_v[k], edge_in[wide, :])
            + mm(pick(send_col[k], grid_rows), grid_proj[...])
            + vector(edge_bias)
        )
        return 0

    lax.fori_loop(0, blocks, first_step, 0)
    loads[6].wait()

    def lane_block(t):
        return lax.rem(4 + t + t * t, 8)

    def twin_block(t):
        return lax.rem(lane_block(t) + 9 - 2 * core, 8)

    def forward_block(k):
        u = first_v[k] + mm(pick(recv_col[k], mesh_rows), rows_a[k])
        hidden, slope = silu_pair(u)
        slope_v[k] = slope.astype(BF16)
        unit, inv = normed(mm(hidden.astype(BF16), edge_out[...]))
        unit_v[k] = unit.astype(BF16)
        inv_v[k] = jnp.broadcast_to(inv, (cap, lanes))
        message = (edge_v[k].astype(F32) + vector(edge_gain) * unit).astype(BF16)
        part_b[k] = mm(put(recv_row[pl.ds(k, 1), :], mesh_rows), message).astype(BF16)

    def backward_block(k):
        wanted = mm(pick(recv_col[k], mesh_rows), rows_c[k])
        wanted_v[k] = wanted.astype(BF16)
        dv = normed_back(wanted * vector(edge_gain), unit_v[k].astype(F32), inv_v[k][:, :1])
        dhidden = mm_t(dv.astype(BF16), edge_out[...])
        dfirst = (dhidden * slope_v[k].astype(F32)).astype(BF16)
        dfirst_v[k] = dfirst
        part_d[k] = mm(put(recv_row[pl.ds(k, 1), :], mesh_rows), dfirst).astype(BF16)

    def all_blocks(block_fn, spread, sums):
        def step(t, _):
            @pl.when(t == 1)
            def _():
                spread_near(*spread)

            @pl.when(t == 2)
            def _():
                sum_near(0, *sums)

            @pl.when(t == 3)
            def _():
                sum_near(1, *sums)
                spread_far(*spread)

            block_fn(lane_block(t))

            @pl.when(t == 3)
            def _():
                sum_far_first(*sums)

            k = twin_block(t)
            spread_arrived(k, *spread)
            block_fn(k)
            pair_copy(k, *sums).start()
            return 0

        lax.fori_loop(0, blocks // 2, step, 0)
        sum_far_last(*sums)

    all_blocks(forward_block, spread_a, sum_b)

    for load in loads[7:10]:
        load.wait()
    node_first[...] = mm(mesh_v[...], node_in[wide, :]) + vector(node_bias)
    aggregate = summed(*sum_b)
    hidden, slope = silu_pair(node_first[...] + mm(aggregate, node_in[mid, :]))
    unit, inv = normed(mm(hidden.astype(BF16), node_out[...]))
    cot = mesh_cot[...].astype(F32)
    dv = normed_back(cot * vector(node_gain), unit, inv)
    dfirst = (mm_t(dv.astype(BF16), node_out[...]) * slope).astype(BF16)
    rows_c[4] = mm_t(dfirst, node_in[mid, :]).astype(BF16)
    spread_own(*spread_c)
    node_mesh_grad[...] = cot + mm_t(dfirst, node_in[wide, :])
    mesh_up[...] = (mesh_v[...].astype(F32) + vector(node_gain) * unit).astype(BF16)
    mesh_up_out = pltpu.make_async_copy(mesh_up, mesh_up_hbm, out_sem.at[blocks])
    mesh_up_out.start()

    for load in loads[10:13]:
        load.wait()

    def grid_step(i, _):
        rows = pl.ds(pl.multiple_of(i * cap, cap), cap)
        own = grid_v[rows, :]
        hidden, slope = silu_pair(mm(own, grid_in[...]) + vector(grid_bias))
        unit, inv = normed(mm(hidden.astype(BF16), grid_out[...]))
        grid_up[rows, :] = (own.astype(F32) + vector(grid_gain) * unit).astype(BF16)
        cot = grid_cot[rows, :].astype(F32)
        dv = normed_back(cot * vector(grid_gain), unit, inv)
        dfirst = (mm_t(dv.astype(BF16), grid_out[...]) * slope).astype(BF16)
        grid_grad[rows, :] = cot + mm_t(dfirst, grid_in[...])
        return 0

    lax.fori_loop(0, grid_rows // cap, grid_step, 0)
    grid_up_out = pltpu.make_async_copy(grid_up, grid_up_hbm, out_sem.at[blocks + 1])
    grid_up_out.start()

    all_blocks(backward_block, spread_c, sum_d)

    def edge_out_copy(k):
        return pltpu.make_async_copy(wanted_v.at[k], grad_edge_hbm.at[0, k], out_sem.at[k])

    def edge_step(k, _):
        wanted_v[k] = (
            wanted_v[k].astype(F32) + mm_t(dfirst_v[k], edge_in[wide, :])
        ).astype(BF16)
        edge_out_copy(k).start()
        return 0

    lax.fori_loop(0, blocks, edge_step, 0)

    def grid_sum_step(i, _):
        start = pl.multiple_of(i * cap, cap)
        rows = pl.ds(start, cap)
        value = mm(put(sender[0, 0:1, :], cap, start), dfirst_v[0])
        for k in range(1, blocks):
            value = value + mm(put(sender[0, k : k + 1, :], cap, start), dfirst_v[k])
        grad_grid[rows, :] = (
            grid_grad[rows, :] + mm_t(value.astype(BF16), edge_in[mid, :])
        ).astype(BF16)
        return 0

    lax.fori_loop(0, grid_rows // cap, grid_sum_step, 0)
    grad_grid_out = pltpu.make_async_copy(grad_grid, grad_grid_hbm, out_sem.at[blocks + 2])
    grad_grid_out.start()

    grad_mesh[...] = (node_mesh_grad[...] + mm_t(summed(*sum_d), edge_in[last, :])).astype(BF16)
    grad_mesh_out = pltpu.make_async_copy(grad_mesh, grad_mesh_hbm, out_sem.at[blocks + 3])
    grad_mesh_out.start()

    spread_sent(*spread_a)
    sum_sent(*sum_b)
    spread_sent(*spread_c)
    sum_sent(*sum_d)
    for k in range(blocks):
        edge_out_copy(k).wait()
    for copy in (mesh_up_out, grid_up_out, grad_grid_out, grad_mesh_out):
        copy.wait()


def on_device(
    grid_latent,
    mesh_latent,
    edge_latent,
    edge_sender,
    edge_receiver,
    edge_count,
    edge_in_weight,
    edge_bias,
    edge_out_weight,
    edge_gain,
    node_in_weight,
    node_bias,
    node_out_weight,
    node_gain,
    grid_in_weight,
    grid_bias,
    grid_out_weight,
    grid_gain,
    mesh_cotangent,
    grid_cotangent,
):
    _, blocks, cap, width = edge_latent.shape
    mesh_rows, grid_rows = mesh_latent.shape[0], grid_latent.shape[0]
    vectors = jnp.stack(
        [edge_bias, edge_gain, node_bias, node_gain, grid_bias, grid_gain]
    ).astype(F32)
    anywhere = pl.BlockSpec(memory_space=pl.ANY)
    vmem = pl.BlockSpec(memory_space=pltpu.VMEM)
    smem = pl.BlockSpec(memory_space=pltpu.SMEM)
    half = blocks // 2 + 1

    def buf(*shape, dtype=BF16):
        return pltpu.VMEM(shape, dtype)

    dma = lambda n: pltpu.SemaphoreType.DMA((n,))
    slots = (blocks, cap, width)
    block = (mesh_rows, width)
    scratch = [
        buf(grid_rows, width),
        buf(mesh_rows, width),
        buf(*slots),
        buf(3 * width, width),
        buf(width, width),
        buf(2 * width, width),
        buf(width, width),
        buf(width, width),
        buf(width, width),
        buf(mesh_rows, width),
        buf(grid_rows, width),
        buf(grid_rows, width),
        buf(blocks, cap, dtype=jnp.int32),
        buf(blocks, cap, 128, dtype=jnp.int32),
        buf(blocks, cap, 128, dtype=jnp.int32),
        buf(*slots, dtype=F32),
        buf(*slots),
        buf(*slots),
        buf(blocks, cap, 128, dtype=F32),
        buf(*slots),
        buf(*slots),
        buf(blocks + 1, *block),
        buf(blocks + 1, *block),
        buf(blocks, *block),
        buf(half, *block),
        buf(4, *block),
        buf(blocks, *block),
        buf(half, *block),
        buf(4, *block),
        buf(*block, dtype=F32),
        buf(*block, dtype=F32),
        buf(grid_rows, width, dtype=F32),
        buf(*block),
        buf(grid_rows, width),
        buf(grid_rows, width),
        buf(*block),
        dma(13),
        dma(blocks + 4),
        dma(8),
        dma(blocks + 1),
        dma(8),
        dma(half),
        dma(4),
        dma(8),
        dma(blocks + 1),
        dma(8),
        dma(half),
        dma(4),
    ]
    outs = [
        jax.ShapeDtypeStruct(mesh_latent.shape, BF16),
        jax.ShapeDtypeStruct(grid_latent.shape, BF16),
        jax.ShapeDtypeStruct(grid_latent.shape, BF16),
        jax.ShapeDtypeStruct(mesh_latent.shape, BF16),
        jax.ShapeDtypeStruct(edge_latent.shape, BF16),
    ]
    return pl.pallas_call(
        functools.partial(kernel, (blocks, cap, width, mesh_rows, grid_rows)),
        out_shape=outs,
        in_specs=[anywhere] * 3 + [vmem, vmem, smem] + [anywhere] * 6 + [vmem] + [anywhere] * 2,
        out_specs=[anywhere] * 5,
        scratch_shapes=scratch,
        compiler_params=pltpu.CompilerParams(
            collective_id=0, has_side_effects=True, vmem_limit_bytes=58 * 2**20
        ),
        cost_estimate=pl.CostEstimate(
            flops=13_000_000_000, bytes_accessed=16_000_000, transcendentals=3_000_000
        ),
        name="encoder",
    )(
        grid_latent,
        mesh_latent,
        edge_latent,
        edge_sender,
        edge_receiver,
        edge_count,
        edge_in_weight,
        edge_out_weight,
        node_in_weight,
        node_out_weight,
        grid_in_weight,
        grid_out_weight,
        vectors,
        mesh_cotangent,
        grid_cotangent,
    )


def solution(mesh):
    rows = P(("grid", "mesh"), None)
    wide = P(("grid", "mesh"), None, None)
    slots = P(("grid", "mesh"), None, None, None)
    return jax.shard_map(
        on_device,
        mesh=mesh,
        in_specs=(rows, rows, slots, wide, wide, rows) + (P(),) * 12 + (rows, rows),
        out_specs=(rows, rows, rows, rows, slots),
        check_vma=False,
    )
```

```python
import functools
from types import SimpleNamespace

import jax
import jax.numpy as jnp
from jax import lax
from jax.experimental import pallas as pl
from jax.experimental.pallas import tpu as pltpu
from jax.sharding import PartitionSpec as P

F32 = jnp.float32
BF16 = jnp.bfloat16
PARTS = 2


def mm(a, b):
    return jnp.dot(a, b, preferred_element_type=F32)


def mm_t(a, b):
    return lax.dot_general(a, b, (((1,), (1,)), ((), ())), preferred_element_type=F32)


def silu_pair(u):
    gate = 0.5 + 0.5 * jnp.tanh(0.5 * u)
    value = u * gate
    return value, gate + value * (1.0 - gate)


def normed(v):
    centred = v - jnp.mean(v, axis=-1, keepdims=True)
    inv = lax.rsqrt(jnp.mean(centred * centred, axis=-1, keepdims=True) + 1e-05)
    return centred * inv, inv


def normed_back(dx, unit, inv):
    along = jnp.mean(dx * unit, axis=-1, keepdims=True)
    return inv * (dx - jnp.mean(dx, axis=-1, keepdims=True) - unit * along)


def kernel(
    sizes,
    grid_hbm,
    mesh_hbm,
    edge_hbm,
    sender,
    receiver,
    count,
    edge_in_hbm,
    edge_out_hbm,
    node_in_hbm,
    node_out_hbm,
    grid_in_hbm,
    grid_out_hbm,
    edge_bias,
    edge_gain,
    node_bias,
    node_gain,
    grid_bias,
    grid_gain,
    mesh_cot_hbm,
    grid_cot_hbm,
    mesh_up_hbm,
    grid_up_hbm,
    grad_grid_hbm,
    grad_mesh_hbm,
    grad_edge_hbm,
    grid_v,
    mesh_v,
    edge_v,
    edge_in,
    edge_out,
    node_in,
    node_out,
    grid_in,
    grid_out,
    mesh_cot,
    grid_cot,
    grid_proj,
    recv_row,
    send_col,
    recv_col,
    first_v,
    slope_v,
    unit_v,
    inv_v,
    wanted_v,
    dfirst_v,
    rows_a,
    rows_c,
    node_first,
    node_mesh_grad,
    grid_grad,
    mesh_up,
    grid_up,
    grad_grid,
    grad_mesh,
    load_sem,
    out_sem,
    a_send,
    a_recv,
    c_send,
    c_recv,
    *sum_refs,
):
    blocks, cap, width, mesh_rows, grid_rows = sizes
    lanes = 128
    fast = lax.axis_size("mesh")
    total = lax.axis_size("grid") * fast
    me = lax.axis_index("grid") * fast + lax.axis_index("mesh")
    core = lax.rem(me, 2)

    def at(shift):
        p = lax.rem(me + (shift + total), total)
        return (lax.div(p, fast), lax.rem(p, fast))

    twin = at(1 - 2 * core)

    def remote(src, dst, send_sem, recv_sem, device):
        return pltpu.make_async_remote_copy(
            src_ref=src,
            dst_ref=dst,
            send_sem=send_sem,
            recv_sem=recv_sem,
            device_id=device,
            device_id_type=pl.DeviceIdType.MESH,
        )

    wide = pl.ds(0, width)
    mid = pl.ds(width, width)
    last = pl.ds(2 * width, width)
    pairs = [
        (mesh_hbm, mesh_v),
        (edge_in_hbm.at[last], edge_in.at[last]),
        (grid_hbm, grid_v),
        (edge_in_hbm.at[mid], edge_in.at[mid]),
        (edge_in_hbm.at[wide], edge_in.at[wide]),
        (edge_hbm.at[0], edge_v),
        (edge_out_hbm, edge_out),
        (node_in_hbm, node_in),
        (node_out_hbm, node_out),
        (mesh_cot_hbm, mesh_cot),
        (grid_in_hbm, grid_in),
        (grid_out_hbm, grid_out),
        (grid_cot_hbm, grid_cot),
    ]
    loads = [pltpu.make_async_copy(src, dst, load_sem.at[i]) for i, (src, dst) in enumerate(pairs)]
    for load in loads[:2]:
        load.start()

    barrier = pltpu.get_barrier_semaphore()
    partners = [at(2), at(-2), at(4), at(-4), at(8), at(-8), twin]
    for partner in partners:
        pl.semaphore_signal(
            barrier, inc=1, device_id=partner, device_id_type=pl.DeviceIdType.MESH
        )

    def vector(ref):
        return ref[...].astype(F32).reshape(1, width)

    def spread_copy(i, part, spread):
        src, dst, device = [
            (4, 2, at(2)),
            (4, 6, at(-2)),
            (4, 3 + 2 * core, twin),
            (2, 0, at(2)),
            (2, 1 + 2 * core, twin),
            (6, 5 + 2 * core, twin),
            (6, 8, at(-2)),
            (8 - 8 * core, 7 - 6 * core, twin),
            (8, 0, at(8)),
        ][i]
        own = part_rows(part)
        return remote(
            spread.rows.at[src, own],
            spread.rows.at[dst, own],
            spread.send.at[i, part],
            spread.recv.at[dst, part],
            device,
        )

    def spread_arrived(slot, part, spread):
        own = spread.rows.at[slot, part_rows(part)]
        remote(own, own, spread.send.at[0, part], spread.recv.at[slot, part], twin).wait_recv()

    def spread_whole(slot, spread):
        for part in range(PARTS):
            spread_arrived(slot, part, spread)

    def spread_own(part, spread):
        for i in (0, 1, 2):
            spread_copy(i, part, spread).start()

    def spread_near(part, spread):
        spread_arrived(2, part, spread)
        spread_arrived(6, part, spread)

        @pl.when(core == 0)
        def _():
            spread_copy(6, part, spread).start()

        @pl.when(core == 1)
        def _():
            spread_copy(3, part, spread).start()

        spread_copy(4, part, spread).start()
        spread_copy(5, part, spread).start()

    def spread_far(part, spread):
        @pl.when(core == 0)
        def _():
            spread_arrived(8, part, spread)
            spread_copy(8, part, spread).start()

        @pl.when(core == 1)
        def _():
            spread_arrived(0, part, spread)

        spread_copy(7, part, spread).start()

    def spread_sent(spread):
        for part in range(PARTS):
            for i in (0, 1, 2, 4, 5, 7):
                spread_copy(i, part, spread).wait_send()

            @pl.when(core == 0)
            def _():
                spread_copy(6, part, spread).wait_send()
                spread_copy(8, part, spread).wait_send()

            @pl.when(core == 1)
            def _():
                spread_copy(3, part, spread).wait_send()

    def pair_copy(k, sums):
        slot = lax.div(k - 1 + 2 * core, 2)
        return remote(
            sums.part.at[k], sums.pair.at[slot], sums.send.at[k], sums.pair_recv.at[slot], twin
        )

    def pair_arrived(slot, sums):
        own = sums.pair.at[slot]
        remote(own, own, sums.send.at[1], sums.pair_recv.at[slot], twin).wait_recv()

    def near_copy(i, sums):
        k, device = [(6, at(2)), (2, at(-2))][i]
        return remote(
            sums.part.at[k], sums.land.at[i], sums.send.at[k], sums.near_recv.at[i], device
        )

    def cross_copy(part, sums):
        own = part_rows(part)
        return remote(
            sums.pair.at[4, own],
            sums.cross.at[own],
            sums.cross_send.at[part],
            sums.cross_recv.at[part],
            at(8),
        )

    def far_copy(part, sums):
        own = part_rows(part)
        return remote(
            sums.part.at[0, own],
            sums.land.at[2, own],
            sums.far_send.at[part],
            sums.far_recv.at[part],
            at(-4),
        )

    def sum_near(i, sums):
        k = (6, 2)[i]
        pair_arrived(k // 2, sums)
        sums.part[k] = (sums.part[k].astype(F32) + sums.pair[k // 2].astype(F32)).astype(BF16)
        near_copy(i, sums).start()

    def sum_cross(sums):
        @pl.when(core == 0)
        def _():
            pair_arrived(4, sums)
            for part in range(PARTS):
                cross_copy(part, sums).start()

    def sum_far(sums):
        def join_part(part, more):
            own = part_rows(part)
            sums.part[0, own] = (sums.part[0, own].astype(F32) + more.astype(F32)).astype(BF16)
            far_copy(part, sums).start()

        @pl.when(core == 0)
        def _():
            for part in range(PARTS):
                cross_copy(part, sums).wait_recv()
                join_part(part, sums.cross[part_rows(part)])

        @pl.when(core == 1)
        def _():
            pair_arrived(0, sums)
            for part in range(PARTS):
                join_part(part, sums.pair[0, part_rows(part)])

    def sum_near_wait(sums):
        pair_arrived(2, sums)
        for i in (0, 1):
            near_copy(i, sums).wait_recv()

    def summed(part, sums):
        far_copy(part, sums).wait_recv()
        own = part_rows(part)
        value = sums.part[4, own].astype(F32) + sums.pair[2, own].astype(F32)
        for i in range(3):
            value = value + sums.land[i, own].astype(F32)
        return value.astype(BF16)

    def sum_sent(sums):
        for k in (1, 3, 5, 7):
            pair_copy(k, sums).wait_send()
        for i in (0, 1):
            near_copy(i, sums).wait_send()
        for part in range(PARTS):
            far_copy(part, sums).wait_send()

        @pl.when(core == 0)
        def _():
            for part in range(PARTS):
                cross_copy(part, sums).wait_send()

    def part_rows(part):
        rows = mesh_rows // PARTS
        return pl.ds(pl.multiple_of(part * rows, rows), rows)

    spread_a = SimpleNamespace(rows=rows_a, send=a_send, recv=a_recv)
    spread_c = SimpleNamespace(rows=rows_c, send=c_send, recv=c_recv)
    sum_b, sum_d = [
        SimpleNamespace(
            part=refs[0],
            pair=refs[1],
            land=refs[2],
            cross=refs[3],
            send=refs[4],
            pair_recv=refs[5],
            near_recv=refs[6],
            far_send=refs[7],
            far_recv=refs[8],
            cross_send=refs[9],
            cross_recv=refs[10],
        )
        for refs in (sum_refs[:11], sum_refs[11:])
    ]

    def pick(column, n):
        tiles = -(-n // lanes)
        ids = jnp.concatenate([column] * tiles, axis=1)[:, :n]
        return jnp.where(lax.broadcasted_iota(jnp.int32, (cap, n), 1) == ids, 1.0, 0.0).astype(BF16)

    def put(row, n, start=0):
        ids = lax.broadcasted_iota(jnp.int32, (n, cap), 0) + start
        return jnp.where(ids == row, 1.0, 0.0).astype(BF16)

    loads[0].wait()
    loads[1].wait()
    for load in loads[2:]:
        load.start()
    rows_a[4] = mm(mesh_v[...], edge_in[last, :]).astype(BF16)
    pl.semaphore_wait(barrier, len(partners))
    for part in range(PARTS):
        spread_own(part, spread_a)

    slot_index = lax.broadcasted_iota(jnp.int32, (1, cap), 1)
    for k in range(blocks):
        recv_row[k : k + 1, :] = jnp.where(slot_index < count[0, k], receiver[0, k : k + 1, :], -1)
    for src, dst in ((sender[0], send_col), (recv_row[...], recv_col)):
        turned = jnp.transpose(src)
        for k in range(blocks):
            dst[k] = jnp.broadcast_to(turned[:, k : k + 1], (cap, lanes))

    for load in loads[2:6]:
        load.wait()
    grid_proj[...] = mm(grid_v[...], edge_in[mid, :]).astype(BF16)

    def first_step(k, _):
        first_v[k] = (
            mm(edge_v[k], edge_in[wide, :])
            + mm(pick(send_col[k], grid_rows), grid_proj[...])
            + vector(edge_bias)
        )
        return 0

    lax.fori_loop(0, blocks, first_step, 0)
    loads[6].wait()

    def step_blocks(t):
        lane = lax.rem(4 + t + t * t, 8)
        other = lax.rem(lane + 9 - 2 * core, 8)
        swap = lax.div(t, 3) * (other - lane)
        return lane + swap, other - swap

    def forward_block(k):
        u = first_v[k] + mm(pick(recv_col[k], mesh_rows), rows_a[k])
        hidden, slope = silu_pair(u)
        slope_v[k] = slope.astype(BF16)
        unit, inv = normed(mm(hidden.astype(BF16), edge_out[...]))
        unit_v[k] = unit.astype(BF16)
        inv_v[k] = jnp.broadcast_to(inv, (cap, lanes))
        message = (edge_v[k].astype(F32) + vector(edge_gain) * unit).astype(BF16)
        sum_b.part[k] = mm(put(recv_row[pl.ds(k, 1), :], mesh_rows), message).astype(BF16)

    def backward_block(k):
        wanted = mm(pick(recv_col[k], mesh_rows), rows_c[k])
        wanted_v[k] = wanted.astype(BF16)
        dv = normed_back(wanted * vector(edge_gain), unit_v[k].astype(F32), inv_v[k][:, :1])
        dhidden = mm_t(dv.astype(BF16), edge_out[...])
        dfirst = (dhidden * slope_v[k].astype(F32)).astype(BF16)
        dfirst_v[k] = dfirst
        sum_d.part[k] = mm(put(recv_row[pl.ds(k, 1), :], mesh_rows), dfirst).astype(BF16)

    def all_blocks(block_fn, spread, sums):
        def step(t, _):
            first, second = step_blocks(t)

            @pl.when(t == 1)
            def _():
                for part in range(PARTS // 2, PARTS):
                    spread_near(part, spread)

            @pl.when(t == 3)
            def _():
                sum_near(0, sums)
                sum_near(1, sums)
                for part in range(PARTS // 2, PARTS):
                    spread_far(part, spread)
                spread_whole(first, spread)

            block_fn(first)

            @pl.when(t == 0)
            def _():
                for part in range(PARTS // 2):
                    spread_near(part, spread)

            @pl.when(t == 2)
            def _():
                for part in range(PARTS // 2):
                    spread_far(part, spread)

            @pl.when(t == 3)
            def _():
                pair_copy(first, sums).start()
                sum_cross(sums)

            @pl.when(jnp.logical_or(t < 3, core == 0))
            def _():
                spread_whole(second, spread)

            block_fn(second)

            @pl.when(t < 3)
            def _():
                pair_copy(second, sums).start()

            return 0

        lax.fori_loop(0, blocks // 2, step, 0)
        sum_far(sums)

    all_blocks(forward_block, spread_a, sum_b)

    def grid_step(i, _):
        rows = pl.ds(pl.multiple_of(i * cap, cap), cap)
        own = grid_v[rows, :]
        hidden, slope = silu_pair(mm(own, grid_in[...]) + vector(grid_bias))
        unit, inv = normed(mm(hidden.astype(BF16), grid_out[...]))
        grid_up[rows, :] = (own.astype(F32) + vector(grid_gain) * unit).astype(BF16)
        cot = grid_cot[rows, :].astype(F32)
        dv = normed_back(cot * vector(grid_gain), unit, inv)
        dfirst = (mm_t(dv.astype(BF16), grid_out[...]) * slope).astype(BF16)
        grid_grad[rows, :] = cot + mm_t(dfirst, grid_in[...])
        return 0

    grid_up_out = pltpu.make_async_copy(grid_up, grid_up_hbm, out_sem.at[blocks + 1])

    def grid_part():
        for load in loads[10:13]:
            load.wait()
        lax.fori_loop(0, grid_rows // cap, grid_step, 0)
        grid_up_out.start()

    for load in loads[7:10]:
        load.wait()
    node_first[...] = mm(mesh_v[...], node_in[wide, :]) + vector(node_bias)
    grid_part()
    sum_near_wait(sum_b)

    def node_step(part, _):
        own = part_rows(part)
        hidden, slope = silu_pair(node_first[own, :] + mm(summed(part, sum_b), node_in[mid, :]))
        unit, inv = normed(mm(hidden.astype(BF16), node_out[...]))
        cot = mesh_cot[own, :].astype(F32)
        dv = normed_back(cot * vector(node_gain), unit, inv)
        dfirst = (mm_t(dv.astype(BF16), node_out[...]) * slope).astype(BF16)
        rows_c[4, own] = mm_t(dfirst, node_in[mid, :]).astype(BF16)
        spread_own(part, spread_c)
        node_mesh_grad[own, :] = cot + mm_t(dfirst, node_in[wide, :])
        mesh_up[own, :] = (mesh_v[own, :].astype(F32) + vector(node_gain) * unit).astype(BF16)
        return 0

    lax.fori_loop(0, PARTS, node_step, 0)
    mesh_up_out = pltpu.make_async_copy(mesh_up, mesh_up_hbm, out_sem.at[blocks])
    mesh_up_out.start()

    all_blocks(backward_block, spread_c, sum_d)

    def edge_out_copy(k):
        return pltpu.make_async_copy(wanted_v.at[k], grad_edge_hbm.at[0, k], out_sem.at[k])

    def edge_step(k, _):
        wanted_v[k] = (
            wanted_v[k].astype(F32) + mm_t(dfirst_v[k], edge_in[wide, :])
        ).astype(BF16)
        edge_out_copy(k).start()
        return 0

    lax.fori_loop(0, blocks, edge_step, 0)

    def grid_sum_step(i, _):
        start = pl.multiple_of(i * cap, cap)
        rows = pl.ds(start, cap)
        value = mm(put(sender[0, 0:1, :], cap, start), dfirst_v[0])
        for k in range(1, blocks):
            value = value + mm(put(sender[0, k : k + 1, :], cap, start), dfirst_v[k])
        grad_grid[rows, :] = (
            grid_grad[rows, :] + mm_t(value.astype(BF16), edge_in[mid, :])
        ).astype(BF16)
        return 0

    lax.fori_loop(0, grid_rows // cap, grid_sum_step, 0)
    grad_grid_out = pltpu.make_async_copy(grad_grid, grad_grid_hbm, out_sem.at[blocks + 2])
    grad_grid_out.start()

    sum_near_wait(sum_d)
    for part in range(PARTS):
        own = part_rows(part)
        grad_mesh[own, :] = (
            node_mesh_grad[own, :] + mm_t(summed(part, sum_d), edge_in[last, :])
        ).astype(BF16)
    grad_mesh_out = pltpu.make_async_copy(grad_mesh, grad_mesh_hbm, out_sem.at[blocks + 3])
    grad_mesh_out.start()

    spread_sent(spread_a)
    sum_sent(sum_b)
    spread_sent(spread_c)
    sum_sent(sum_d)
    for k in range(blocks):
        edge_out_copy(k).wait()
    for copy in (mesh_up_out, grid_up_out, grad_grid_out, grad_mesh_out):
        copy.wait()


def place_kernel(*refs):
    sources, targets, held, load_sem, store_sem = refs[:5], refs[5:10], refs[10:15], refs[15], refs[16]
    views = [lambda ref, k=k: ref.at[0, k] for k in range(sources[4].shape[1])]
    work = [(4, view) for view in views] + [(i, lambda ref: ref) for i in (1, 2, 0, 3)]
    loads, stores = [], []
    for n, (i, view) in enumerate(work):
        loads.append(pltpu.make_async_copy(view(sources[i]), view(held[i]), load_sem.at[n]))
        stores.append(pltpu.make_async_copy(view(held[i]), view(targets[i]), store_sem.at[n]))
    for load in loads:
        load.start()
    for load, store in zip(loads, stores):
        load.wait()
        store.start()
    for store in stores:
        store.wait()


def on_device(
    grid_latent,
    mesh_latent,
    edge_latent,
    edge_sender,
    edge_receiver,
    edge_count,
    edge_in_weight,
    edge_bias,
    edge_out_weight,
    edge_gain,
    node_in_weight,
    node_bias,
    node_out_weight,
    node_gain,
    grid_in_weight,
    grid_bias,
    grid_out_weight,
    grid_gain,
    mesh_cotangent,
    grid_cotangent,
):
    _, blocks, cap, width = edge_latent.shape
    mesh_rows, grid_rows = mesh_latent.shape[0], grid_latent.shape[0]
    anywhere = pl.BlockSpec(memory_space=pl.ANY)
    vmem = pl.BlockSpec(memory_space=pltpu.VMEM)
    smem = pl.BlockSpec(memory_space=pltpu.SMEM)

    def buf(*shape, dtype=BF16):
        return pltpu.VMEM(shape, dtype)

    dma = pltpu.SemaphoreType.DMA
    slots = (blocks, cap, width)
    block = (mesh_rows, width)
    scratch = [
        buf(grid_rows, width),
        buf(mesh_rows, width),
        buf(*slots),
        buf(3 * width, width),
        buf(width, width),
        buf(2 * width, width),
        buf(width, width),
        buf(width, width),
        buf(width, width),
        buf(mesh_rows, width),
        buf(grid_rows, width),
        buf(grid_rows, width),
        buf(blocks, cap, dtype=jnp.int32),
        buf(blocks, cap, 128, dtype=jnp.int32),
        buf(blocks, cap, 128, dtype=jnp.int32),
        buf(*slots, dtype=F32),
        buf(*slots),
        buf(*slots),
        buf(blocks, cap, 128, dtype=F32),
        buf(*slots),
        buf(*slots),
        buf(blocks + 1, *block),
        buf(blocks + 1, *block),
        buf(*block, dtype=F32),
        buf(*block, dtype=F32),
        buf(grid_rows, width, dtype=F32),
        buf(*block),
        buf(grid_rows, width),
        buf(grid_rows, width),
        buf(*block),
        dma((13,)),
        dma((blocks + 4,)),
        dma((9, PARTS)),
        dma((blocks + 1, PARTS)),
        dma((9, PARTS)),
        dma((blocks + 1, PARTS)),
    ]
    sums = [
        buf(blocks, *block),
        buf(blocks // 2 + 1, *block),
        buf(3, *block),
        buf(*block),
        dma((blocks,)),
        dma((blocks // 2 + 1,)),
        dma((2,)),
        dma((PARTS,)),
        dma((PARTS,)),
        dma((PARTS,)),
        dma((PARTS,)),
    ]
    scratch = scratch + sums + sums
    outs = [
        jax.ShapeDtypeStruct(mesh_latent.shape, BF16),
        jax.ShapeDtypeStruct(grid_latent.shape, BF16),
        jax.ShapeDtypeStruct(grid_latent.shape, BF16),
        jax.ShapeDtypeStruct(mesh_latent.shape, BF16),
        jax.ShapeDtypeStruct(edge_latent.shape, BF16),
    ]
    results = pl.pallas_call(
        functools.partial(kernel, (blocks, cap, width, mesh_rows, grid_rows)),
        out_shape=outs,
        in_specs=[anywhere] * 3 + [vmem, vmem, smem] + [anywhere] * 6 + [vmem] * 6 + [anywhere] * 2,
        out_specs=[anywhere] * 5,
        scratch_shapes=scratch,
        compiler_params=pltpu.CompilerParams(
            collective_id=0, has_side_effects=True, vmem_limit_bytes=58 * 2**20
        ),
        cost_estimate=pl.CostEstimate(
            flops=13_000_000_000, bytes_accessed=16_000_000, transcendentals=3_000_000
        ),
        name="encoder",
    )(
        grid_latent,
        mesh_latent,
        edge_latent,
        edge_sender,
        edge_receiver,
        edge_count,
        edge_in_weight,
        edge_out_weight,
        node_in_weight,
        node_out_weight,
        grid_in_weight,
        grid_out_weight,
        edge_bias,
        edge_gain,
        node_bias,
        node_gain,
        grid_bias,
        grid_gain,
        mesh_cotangent,
        grid_cotangent,
    )
    return pl.pallas_call(
        place_kernel,
        out_shape=outs,
        in_specs=[anywhere] * 5,
        out_specs=[anywhere] * 5,
        scratch_shapes=[pltpu.VMEM(out.shape, out.dtype) for out in outs]
        + [dma((blocks + 4,)), dma((blocks + 4,))],
        compiler_params=pltpu.CompilerParams(vmem_limit_bytes=60 * 2**20),
        name="place",
    )(*results)


def solution(mesh):
    rows = P(("grid", "mesh"), None)
    wide = P(("grid", "mesh"), None, None)
    slots = P(("grid", "mesh"), None, None, None)
    return jax.shard_map(
        on_device,
        mesh=mesh,
        in_specs=(rows, rows, slots, wide, wide, rows) + (P(),) * 12 + (rows, rows),
        out_specs=(rows, rows, rows, rows, slots),
        check_vma=False,
    )
```

```python
import functools
from types import SimpleNamespace

import jax
import jax.numpy as jnp
from jax import lax
from jax.experimental import pallas as pl
from jax.experimental.pallas import tpu as pltpu
from jax.sharding import PartitionSpec as P

F32 = jnp.float32
BF16 = jnp.bfloat16
PARTS = 2


def mm(a, b):
    return jnp.dot(a, b, preferred_element_type=F32)


def mm_t(a, b):
    return lax.dot_general(a, b, (((1,), (1,)), ((), ())), preferred_element_type=F32)


def silu_pair(u):
    gate = 0.5 + 0.5 * jnp.tanh(0.5 * u)
    value = u * gate
    return value, gate + value * (1.0 - gate)


def normed(v):
    centred = v - jnp.mean(v, axis=-1, keepdims=True)
    inv = lax.rsqrt(jnp.mean(centred * centred, axis=-1, keepdims=True) + 1e-05)
    return centred * inv, inv


def normed_back(dx, unit, inv):
    along = jnp.mean(dx * unit, axis=-1, keepdims=True)
    return inv * (dx - jnp.mean(dx, axis=-1, keepdims=True) - unit * along)


def kernel(
    sizes,
    grid_hbm,
    mesh_hbm,
    edge_hbm,
    sender_hbm,
    receiver_hbm,
    count_hbm,
    edge_in_hbm,
    edge_out_hbm,
    node_in_hbm,
    node_out_hbm,
    grid_in_hbm,
    grid_out_hbm,
    edge_bias_hbm,
    edge_gain_hbm,
    node_bias_hbm,
    node_gain_hbm,
    grid_bias_hbm,
    grid_gain_hbm,
    mesh_cot_hbm,
    grid_cot_hbm,
    mesh_up_hbm,
    grid_up_hbm,
    grad_grid_hbm,
    grad_mesh_hbm,
    grad_edge_hbm,
    sender,
    receiver,
    count,
    edge_bias,
    edge_gain,
    node_bias,
    node_gain,
    grid_bias,
    grid_gain,
    grid_v,
    edge_v,
    edge_in,
    edge_out,
    node_in,
    node_out,
    grid_in,
    grid_out,
    mesh_cot,
    grid_cot,
    grid_proj,
    recv_row,
    lent_row,
    send_col,
    recv_col,
    first_v,
    slope_v,
    unit_v,
    inv_v,
    wanted_v,
    dfirst_v,
    rows_a,
    rows_c,
    node_first,
    node_mesh_grad,
    grid_grad,
    grid_sum,
    mesh_up,
    grid_up,
    grad_grid,
    grad_mesh,
    load_sem,
    out_sem,
    a_send,
    a_recv,
    c_send,
    c_recv,
    lend_send,
    lend_recv,
    *sum_refs,
):
    blocks, cap, width, mesh_rows, grid_rows = sizes
    lanes = 128
    fast = lax.axis_size("mesh")
    total = lax.axis_size("grid") * fast
    me = lax.axis_index("grid") * fast + lax.axis_index("mesh")
    core = lax.rem(me, 2)

    def at(shift):
        p = lax.rem(me + (shift + total), total)
        return (lax.div(p, fast), lax.rem(p, fast))

    twin = at(1 - 2 * core)

    def remote(src, dst, send_sem, recv_sem, device):
        return pltpu.make_async_remote_copy(
            src_ref=src,
            dst_ref=dst,
            send_sem=send_sem,
            recv_sem=recv_sem,
            device_id=device,
            device_id_type=pl.DeviceIdType.MESH,
        )

    wide = pl.ds(0, width)
    mid = pl.ds(width, width)
    last = pl.ds(2 * width, width)
    pairs = [
        (grid_hbm, grid_v),
        (edge_in_hbm.at[mid], edge_in.at[mid]),
        (edge_in_hbm.at[wide], edge_in.at[wide]),
        (edge_hbm.at[0], edge_v.at[pl.ds(0, blocks)]),
        (edge_in_hbm.at[last], edge_in.at[last]),
        (mesh_hbm, rows_a.at[4]),
        (edge_out_hbm, edge_out),
        (node_in_hbm, node_in),
        (node_out_hbm, node_out),
        (mesh_cot_hbm, mesh_cot),
        (grid_in_hbm, grid_in),
        (grid_out_hbm, grid_out),
        (grid_cot_hbm, grid_cot),
    ]
    small = [
        (count_hbm, count),
        (sender_hbm, sender),
        (receiver_hbm, receiver),
        (edge_bias_hbm, edge_bias),
        (edge_gain_hbm, edge_gain),
        (node_bias_hbm, node_bias),
        (node_gain_hbm, node_gain),
        (grid_bias_hbm, grid_bias),
        (grid_gain_hbm, grid_gain),
    ]
    few = [
        pltpu.make_async_copy(src, dst, load_sem.at[len(pairs) + i])
        for i, (src, dst) in enumerate(small)
    ]
    loads = [pltpu.make_async_copy(src, dst, load_sem.at[i]) for i, (src, dst) in enumerate(pairs)]
    barrier = pltpu.get_barrier_semaphore()
    partners = [at(2), at(-2), at(8), at(-8), twin]
    for partner in partners:
        pl.semaphore_signal(
            barrier, inc=1, device_id=partner, device_id_type=pl.DeviceIdType.MESH
        )

    def vector(ref):
        return ref[...].astype(F32).reshape(1, width)

    def part_rows(part):
        rows = mesh_rows // PARTS
        return pl.ds(pl.multiple_of(part * rows, rows), rows)

    far = 8 - 8 * core
    onward = 2 - 4 * core

    def spread_copy(i, part, spread):
        src, dst, device = [
            (4, 2, at(2)),
            (4, 6, at(-2)),
            (4, 3 + 2 * core, twin),
            (2 + 4 * (1 - core), far, at(-onward)),
            (2, 1 + 2 * core, twin),
            (6, 5 + 2 * core, twin),
            (far, 7 - 6 * core, twin),
        ][i]
        own = part_rows(part)
        return remote(
            spread.own.at[own] if i < 3 else spread.rows.at[src, own],
            spread.rows.at[dst, own],
            spread.send.at[i, part],
            spread.recv.at[dst, part],
            device,
        )

    def spread_arrived(slot, part, spread):
        own = spread.rows.at[slot, part_rows(part)]
        remote(own, own, spread.send.at[0, part], spread.recv.at[slot, part], twin).wait_recv()

    def spread_whole(slot, spread):
        for part in range(PARTS):
            spread_arrived(slot, part, spread)

    def spread_own(part, spread):
        for i in (0, 1, 2):
            spread_copy(i, part, spread).start()

    def spread_near(part, spread):
        spread_arrived(2, part, spread)
        spread_arrived(6, part, spread)
        for i in (3, 4, 5):
            spread_copy(i, part, spread).start()

    def spread_far(part, spread):
        spread_arrived(far, part, spread)
        spread_copy(6, part, spread).start()

    def spread_sent(spread):
        for part in range(PARTS):
            for i in range(7):
                spread_copy(i, part, spread).wait_send()

    def pair_copy(k, sums):
        slot = lax.div(k - 1 + 2 * core, 2)
        return remote(
            sums.part.at[k], sums.pair.at[slot], sums.pair_send.at[k], sums.pair_recv.at[slot], twin
        )

    def pair_arrived(slot, sums):
        own = sums.pair.at[slot]
        remote(own, own, sums.pair_send.at[1], sums.pair_recv.at[slot], twin).wait_recv()

    early = 2 + 4 * core
    late = 6 - 4 * core

    def early_copy(part, sums):
        own = part_rows(part)
        return remote(
            sums.part.at[early, own],
            sums.land.at[1 - core, own],
            sums.send.at[0, part],
            sums.land_recv.at[1 - core, part],
            at(-onward),
        )

    def late_copy(part, sums):
        own = part_rows(part)
        return remote(
            sums.part.at[late, own],
            sums.land.at[core, own],
            sums.send.at[1, part],
            sums.land_recv.at[core, part],
            at(onward),
        )

    def far_copy(part, sums):
        own = part_rows(part)
        return remote(
            sums.part.at[far, own],
            sums.cross.at[own],
            sums.send.at[2, part],
            sums.cross_recv.at[part],
            at(onward),
        )

    def join(k, own, sums, *more):
        value = sums.part[k, own].astype(F32) + sums.pair[lax.div(k, 2), own].astype(F32)
        for other in more:
            value = value + other.astype(F32)
        sums.part[k, own] = value.astype(BF16)

    def sum_early(sums):
        pair_arrived(lax.div(early, 2), sums)
        for part in range(PARTS):
            join(early, part_rows(part), sums)
            early_copy(part, sums).start()

    def sum_far(sums):
        pair_arrived(lax.div(far, 2), sums)
        for part in range(PARTS):
            join(far, part_rows(part), sums)
            far_copy(part, sums).start()

    def sum_late(sums):
        pair_arrived(lax.div(late, 2), sums)
        pair_arrived(2, sums)
        for part in range(PARTS):
            own = part_rows(part)
            far_copy(part, sums).wait_recv()
            join(late, own, sums, sums.cross[own])
            late_copy(part, sums).start()

    def summed(part, sums):
        own = part_rows(part)
        early_copy(part, sums).wait_recv()
        late_copy(part, sums).wait_recv()
        value = sums.part[4, own].astype(F32) + sums.pair[2, own].astype(F32)
        return (value + sums.land[0, own].astype(F32) + sums.land[1, own].astype(F32)).astype(BF16)

    def sum_sent(sums):
        for k in (1, 3, 5, 7):
            pair_copy(k, sums).wait_send()
        for part in range(PARTS):
            for copy in (early_copy, late_copy, far_copy):
                copy(part, sums).wait_send()

    spread_a = SimpleNamespace(own=mesh_hbm, rows=rows_a, send=a_send, recv=a_recv)
    spread_c = SimpleNamespace(own=rows_c.at[4], rows=rows_c, send=c_send, recv=c_recv)
    sum_b, sum_d = [
        SimpleNamespace(
            part=refs[0],
            pair=refs[1],
            land=refs[2],
            cross=refs[3],
            pair_send=refs[4],
            pair_recv=refs[5],
            send=refs[6],
            land_recv=refs[7],
            cross_recv=refs[8],
        )
        for refs in (sum_refs[:9], sum_refs[9:])
    ]

    def lend_copy(i):
        src, dst, shift = [
            (edge_v.at[0], edge_v.at[blocks], -8),
            (first_v.at[0], first_v.at[blocks], -8),
            (recv_row.at[pl.ds(0, blocks)], lent_row, -8),
            (wanted_v.at[blocks], wanted_v.at[0], 8),
            (dfirst_v.at[blocks], dfirst_v.at[0], 8),
        ][i]
        return remote(src, dst, lend_send.at[i], lend_recv.at[i], at(shift))

    def on_even(*steps):
        @pl.when(core == 0)
        def _():
            for step in steps:
                step()

    def pick(column, n):
        tiles = -(-n // lanes)
        ids = jnp.concatenate([column] * tiles, axis=1)[:, :n]
        return jnp.where(lax.broadcasted_iota(jnp.int32, (cap, n), 1) == ids, 1.0, 0.0).astype(BF16)

    def put(row, n, start=0):
        ids = lax.broadcasted_iota(jnp.int32, (n, cap), 0) + start
        return jnp.where(ids == row, 1.0, 0.0).astype(BF16)

    for load in few:
        load.start()
    pl.semaphore_wait(barrier, len(partners))
    for part in range(PARTS):
        spread_own(part, spread_a)
    for load in loads:
        load.start()

    for load in few:
        load.wait()

    slot_index = lax.broadcasted_iota(jnp.int32, (1, cap), 1)
    for k in range(blocks):
        recv_row[k : k + 1, :] = jnp.where(slot_index < count[0, k], receiver[0, k : k + 1, :], -1)
    on_even(lend_copy(2).start)
    for src, dst in ((sender[0], send_col), (recv_row[:blocks, :], recv_col)):
        turned = jnp.transpose(src)
        for k in range(blocks):
            dst[k] = jnp.broadcast_to(turned[:, k : k + 1], (cap, lanes))

    for load in loads[:4]:
        load.wait()
    on_even(lend_copy(0).start)
    grid_proj[...] = mm(grid_v[...], edge_in[mid, :]).astype(BF16)

    def first_step(k, _):
        first_v[k] = (
            mm(edge_v[k], edge_in[wide, :])
            + mm(pick(send_col[k], grid_rows), grid_proj[...])
            + vector(edge_bias)
        ).astype(BF16)

        @pl.when(jnp.logical_and(k == 0, core == 0))
        def _():
            lend_copy(1).start()

        return 0

    lax.fori_loop(0, blocks // 2, first_step, 0)
    for part in range(PARTS // 2):
        spread_near(part, spread_a)
    lax.fori_loop(blocks // 2, blocks, first_step, 0)
    for load in loads[4:7]:
        load.wait()

    def step_blocks(t, swap):
        lane = lax.rem(4 + t + t * t, 8)
        other = lax.rem(lane + 9 - 2 * core, 8)
        lane = lane + lax.div(t, 3) * far
        move = (lax.div(t, 3) * (1 - core) if swap else 0) * (other - lane)
        return lane + move, other - move

    def forward_block(k):
        joined = mm(pick(recv_col[k], mesh_rows), rows_a[k]).astype(BF16)
        u = first_v[k].astype(F32) + mm(joined, edge_in[last, :])
        hidden, slope = silu_pair(u)
        slope_v[k] = slope.astype(BF16)
        unit, inv = normed(mm(hidden.astype(BF16), edge_out[...]))
        unit_v[k] = unit.astype(BF16)
        inv_v[k] = jnp.broadcast_to(inv, (cap, lanes))
        message = (edge_v[k].astype(F32) + vector(edge_gain) * unit).astype(BF16)
        sum_b.part[k] = mm(put(recv_row[pl.ds(k, 1), :], mesh_rows), message).astype(BF16)

    def backward_block(k):
        wanted = mm(pick(recv_col[k], mesh_rows), rows_c[k])
        wanted_v[k] = wanted.astype(BF16)
        dv = normed_back(wanted * vector(edge_gain), unit_v[k].astype(F32), inv_v[k][:, :1])
        dhidden = mm_t(dv.astype(BF16), edge_out[...])
        dfirst = (dhidden * slope_v[k].astype(F32)).astype(BF16)
        dfirst_v[k] = dfirst
        sum_d.part[k] = mm(put(recv_row[pl.ds(k, 1), :], mesh_rows), dfirst).astype(BF16)

    def all_blocks(block_fn, spread, sums, after_own, before_lent, after_lent, swap):
        def step(t, _):
            first, second = step_blocks(t, swap)

            @pl.when(t == 1)
            def _():
                for part in range(PARTS // 2, PARTS):
                    spread_near(part, spread)

            @pl.when(t == 3)
            def _():
                sum_early(sums)
                for part in range(PARTS // 2, PARTS):
                    spread_far(part, spread)
                if swap:
                    on_even(functools.partial(spread_whole, 1, spread))
                else:
                    on_even(*before_lent)

            block_fn(first)

            @pl.when(t == 0)
            def _():
                for step in after_own:
                    step()

            @pl.when(t == 2)
            def _():
                for part in range(PARTS // 2):
                    spread_far(part, spread)

            @pl.when(t == 3)
            def _():
                if swap:
                    on_even(pair_copy(1, sums).start, *before_lent)
                else:
                    on_even(*after_lent)

            twin_second = jnp.logical_or(t < 3, core == 1) if swap else t >= 0

            @pl.when(twin_second)
            def _():
                spread_whole(second, spread)

            block_fn(second)

            @pl.when(twin_second)
            def _():
                pair_copy(second, sums).start()

            return 0

        lax.fori_loop(0, blocks // 2, step, 0)
        sum_far(sums)

    def lent_columns():
        recv_row[blocks : blocks + 1, :] = lent_row[0:1, :]
        turned = jnp.transpose(lent_row[...])
        recv_col[blocks] = jnp.broadcast_to(turned[:, 0:1], (cap, lanes))

    all_blocks(
        forward_block,
        spread_a,
        sum_b,
        [],
        [lend_copy(i).wait_recv for i in (0, 1, 2)] + [lent_columns],
        [],
        True,
    )

    def grid_step(i, _):
        rows = pl.ds(pl.multiple_of(i * cap, cap), cap)
        own = grid_v[rows, :]
        hidden, slope = silu_pair(mm(own, grid_in[...]) + vector(grid_bias))
        unit, inv = normed(mm(hidden.astype(BF16), grid_out[...]))
        grid_up[rows, :] = (own.astype(F32) + vector(grid_gain) * unit).astype(BF16)
        cot = grid_cot[rows, :].astype(F32)
        dv = normed_back(cot * vector(grid_gain), unit, inv)
        dfirst = (mm_t(dv.astype(BF16), grid_out[...]) * slope).astype(BF16)
        grid_grad[rows, :] = cot + mm_t(dfirst, grid_in[...])
        return 0

    grid_up_out = pltpu.make_async_copy(grid_up, grid_up_hbm, out_sem.at[blocks + 1])

    def grid_part():
        for load in loads[10:13]:
            load.wait()
        lax.fori_loop(0, grid_rows // cap, grid_step, 0)
        grid_up_out.start()

    for load in loads[7:10]:
        load.wait()
    node_first[...] = mm(rows_a[4], node_in[wide, :]) + vector(node_bias)
    grid_part()
    sum_late(sum_b)

    def node_step(part, _):
        own = part_rows(part)
        hidden, slope = silu_pair(node_first[own, :] + mm(summed(part, sum_b), node_in[mid, :]))
        unit, inv = normed(mm(hidden.astype(BF16), node_out[...]))
        cot = mesh_cot[own, :].astype(F32)
        dv = normed_back(cot * vector(node_gain), unit, inv)
        dfirst = (mm_t(dv.astype(BF16), node_out[...]) * slope).astype(BF16)
        rows_c[4, own] = mm_t(dfirst, node_in[mid, :]).astype(BF16)
        spread_own(part, spread_c)
        node_mesh_grad[own, :] = cot + mm_t(dfirst, node_in[wide, :])
        mesh_up[own, :] = (rows_a[4, own].astype(F32) + vector(node_gain) * unit).astype(BF16)
        return 0

    lax.fori_loop(0, PARTS, node_step, 0)
    mesh_up_out = pltpu.make_async_copy(mesh_up, mesh_up_hbm, out_sem.at[blocks])
    mesh_up_out.start()

    all_blocks(
        backward_block,
        spread_c,
        sum_d,
        [functools.partial(spread_near, part, spread_c) for part in range(PARTS // 2)],
        [],
        [lend_copy(3).start, lend_copy(4).start],
        False,
    )

    def edge_out_copy(k):
        return pltpu.make_async_copy(wanted_v.at[k], grad_edge_hbm.at[0, k], out_sem.at[k])

    def edge_step(i, _):
        k = lax.rem(i + 1, blocks)
        wanted_v[k] = (
            wanted_v[k].astype(F32) + mm_t(dfirst_v[k], edge_in[wide, :])
        ).astype(BF16)
        edge_out_copy(k).start()
        return 0

    def grid_sum_step(i, _):
        start = pl.multiple_of(i * cap, cap)
        value = mm(put(sender[0, 1:2, :], cap, start), dfirst_v[1])
        for k in range(2, blocks):
            value = value + mm(put(sender[0, k : k + 1, :], cap, start), dfirst_v[k])
        grid_sum[pl.ds(start, cap), :] = value
        return 0

    def grid_last_step(i, _):
        start = pl.multiple_of(i * cap, cap)
        rows = pl.ds(start, cap)
        value = grid_sum[rows, :] + mm(put(sender[0, 0:1, :], cap, start), dfirst_v[0])
        grad_grid[rows, :] = (
            grid_grad[rows, :] + mm_t(value.astype(BF16), edge_in[mid, :])
        ).astype(BF16)
        return 0

    lax.fori_loop(0, blocks - 1, edge_step, 0)
    sum_late(sum_d)
    lax.fori_loop(0, grid_rows // cap, grid_sum_step, 0)
    on_even(lend_copy(3).wait_recv, lend_copy(4).wait_recv)
    lax.fori_loop(blocks - 1, blocks, edge_step, 0)
    lax.fori_loop(0, grid_rows // cap, grid_last_step, 0)
    grad_grid_out = pltpu.make_async_copy(grad_grid, grad_grid_hbm, out_sem.at[blocks + 2])
    grad_grid_out.start()

    for part in range(PARTS):
        own = part_rows(part)
        grad_mesh[own, :] = (
            node_mesh_grad[own, :] + mm_t(summed(part, sum_d), edge_in[last, :])
        ).astype(BF16)
    grad_mesh_out = pltpu.make_async_copy(grad_mesh, grad_mesh_hbm, out_sem.at[blocks + 3])
    grad_mesh_out.start()

    spread_sent(spread_a)
    sum_sent(sum_b)
    spread_sent(spread_c)
    sum_sent(sum_d)
    on_even(*[lend_copy(i).wait_send for i in range(5)])
    for k in range(blocks):
        edge_out_copy(k).wait()
    for copy in (mesh_up_out, grid_up_out, grad_grid_out, grad_mesh_out):
        copy.wait()


def place_kernel(*refs):
    sources, targets, held, load_sem, store_sem = refs[:5], refs[5:10], refs[10:15], refs[15], refs[16]
    views = [lambda ref, k=k: ref.at[0, k] for k in range(sources[4].shape[1])]
    work = [(4, view) for view in views] + [(i, lambda ref: ref) for i in (1, 2, 0, 3)]
    loads, stores = [], []
    for n, (i, view) in enumerate(work):
        loads.append(pltpu.make_async_copy(view(sources[i]), view(held[i]), load_sem.at[n]))
        stores.append(pltpu.make_async_copy(view(held[i]), view(targets[i]), store_sem.at[n]))
    for load in loads:
        load.start()
    for load, store in zip(loads, stores):
        load.wait()
        store.start()
    for store in stores:
        store.wait()


def on_device(
    grid_latent,
    mesh_latent,
    edge_latent,
    edge_sender,
    edge_receiver,
    edge_count,
    edge_in_weight,
    edge_bias,
    edge_out_weight,
    edge_gain,
    node_in_weight,
    node_bias,
    node_out_weight,
    node_gain,
    grid_in_weight,
    grid_bias,
    grid_out_weight,
    grid_gain,
    mesh_cotangent,
    grid_cotangent,
):
    _, blocks, cap, width = edge_latent.shape
    mesh_rows, grid_rows = mesh_latent.shape[0], grid_latent.shape[0]
    anywhere = pl.BlockSpec(memory_space=pl.ANY)

    def buf(*shape, dtype=BF16):
        return pltpu.VMEM(shape, dtype)

    dma = pltpu.SemaphoreType.DMA
    more_slots = (blocks + 1, cap, width)
    block = (mesh_rows, width)
    scratch = [
        buf(*edge_sender.shape, dtype=jnp.int32),
        buf(*edge_receiver.shape, dtype=jnp.int32),
        pltpu.SMEM(edge_count.shape, jnp.int32),
        buf(width),
        buf(width),
        buf(width),
        buf(width),
        buf(width),
        buf(width),
        buf(grid_rows, width),
        buf(*more_slots),
        buf(3 * width, width),
        buf(width, width),
        buf(2 * width, width),
        buf(width, width),
        buf(width, width),
        buf(width, width),
        buf(mesh_rows, width),
        buf(grid_rows, width),
        buf(grid_rows, width),
        buf(2 * blocks, cap, dtype=jnp.int32),
        buf(blocks, cap, dtype=jnp.int32),
        buf(blocks, cap, 128, dtype=jnp.int32),
        buf(blocks + 1, cap, 128, dtype=jnp.int32),
        buf(*more_slots),
        buf(*more_slots),
        buf(*more_slots),
        buf(blocks + 1, cap, 128, dtype=F32),
        buf(*more_slots),
        buf(*more_slots),
        buf(blocks + 1, *block),
        buf(blocks + 1, *block),
        buf(*block, dtype=F32),
        buf(*block, dtype=F32),
        buf(grid_rows, width, dtype=F32),
        buf(grid_rows, width, dtype=F32),
        buf(*block),
        buf(grid_rows, width),
        buf(grid_rows, width),
        buf(*block),
        dma((22,)),
        dma((blocks + 4,)),
        dma((7, PARTS)),
        dma((blocks + 1, PARTS)),
        dma((7, PARTS)),
        dma((blocks + 1, PARTS)),
        dma((5,)),
        dma((5,)),
    ]
    sums = [
        buf(blocks + 1, *block),
        buf(blocks // 2 + 1, *block),
        buf(2, *block),
        buf(*block),
        dma((blocks,)),
        dma((blocks // 2 + 1,)),
        dma((3, PARTS)),
        dma((2, PARTS)),
        dma((PARTS,)),
    ]
    scratch = scratch + sums + sums
    outs = [
        jax.ShapeDtypeStruct(mesh_latent.shape, BF16),
        jax.ShapeDtypeStruct(grid_latent.shape, BF16),
        jax.ShapeDtypeStruct(grid_latent.shape, BF16),
        jax.ShapeDtypeStruct(mesh_latent.shape, BF16),
        jax.ShapeDtypeStruct(edge_latent.shape, BF16),
    ]
    results = pl.pallas_call(
        functools.partial(kernel, (blocks, cap, width, mesh_rows, grid_rows)),
        out_shape=outs,
        in_specs=[anywhere] * 20,
        out_specs=[anywhere] * 5,
        scratch_shapes=scratch,
        compiler_params=pltpu.CompilerParams(
            collective_id=0, has_side_effects=True, vmem_limit_bytes=58 * 2**20
        ),
        cost_estimate=pl.CostEstimate(
            flops=13_000_000_000, bytes_accessed=16_000_000, transcendentals=3_000_000
        ),
        name="encoder",
    )(
        grid_latent,
        mesh_latent,
        edge_latent,
        edge_sender,
        edge_receiver,
        edge_count,
        edge_in_weight,
        edge_out_weight,
        node_in_weight,
        node_out_weight,
        grid_in_weight,
        grid_out_weight,
        edge_bias,
        edge_gain,
        node_bias,
        node_gain,
        grid_bias,
        grid_gain,
        mesh_cotangent,
        grid_cotangent,
    )
    return pl.pallas_call(
        place_kernel,
        out_shape=outs,
        in_specs=[anywhere] * 5,
        out_specs=[anywhere] * 5,
        scratch_shapes=[pltpu.VMEM(out.shape, out.dtype) for out in outs]
        + [dma((blocks + 4,)), dma((blocks + 4,))],
        compiler_params=pltpu.CompilerParams(vmem_limit_bytes=60 * 2**20),
        name="place",
    )(*results)


def solution(mesh):
    rows = P(("grid", "mesh"), None)
    wide = P(("grid", "mesh"), None, None)
    slots = P(("grid", "mesh"), None, None, None)
    return jax.shard_map(
        on_device,
        mesh=mesh,
        in_specs=(rows, rows, slots, wide, wide, rows) + (P(),) * 12 + (rows, rows),
        out_specs=(rows, rows, rows, rows, slots),
        check_vma=False,
    )
```

```python
import functools
from types import SimpleNamespace

import jax
import jax.numpy as jnp
from jax import lax
from jax.experimental import pallas as pl
from jax.experimental.pallas import tpu as pltpu
from jax.sharding import PartitionSpec as P

F32 = jnp.float32
BF16 = jnp.bfloat16
PARTS = 2


def mm(a, b):
    return jnp.dot(a, b, preferred_element_type=F32)


def mm_t(a, b):
    return lax.dot_general(a, b, (((1,), (1,)), ((), ())), preferred_element_type=F32)


def silu_pair(u):
    gate = 0.5 + 0.5 * jnp.tanh(0.5 * u)
    value = u * gate
    return value, gate + value * (1.0 - gate)


def normed(v):
    centred = v - jnp.mean(v, axis=-1, keepdims=True)
    inv = lax.rsqrt(jnp.mean(centred * centred, axis=-1, keepdims=True) + 1e-05)
    return centred * inv, inv


def normed_back(dx, unit, inv):
    along = jnp.mean(dx * unit, axis=-1, keepdims=True)
    return inv * (dx - jnp.mean(dx, axis=-1, keepdims=True) - unit * along)


def kernel(
    sizes,
    grid_hbm,
    mesh_hbm,
    edge_hbm,
    sender_hbm,
    receiver_hbm,
    count_hbm,
    edge_in_hbm,
    edge_out_hbm,
    node_in_hbm,
    node_out_hbm,
    grid_in_hbm,
    grid_out_hbm,
    edge_bias_hbm,
    edge_gain_hbm,
    node_bias_hbm,
    node_gain_hbm,
    grid_bias_hbm,
    grid_gain_hbm,
    mesh_cot_hbm,
    grid_cot_hbm,
    mesh_up,
    grid_up,
    grad_grid,
    grad_mesh,
    grad_edge,
    sender,
    receiver,
    count,
    edge_bias,
    edge_gain,
    node_bias,
    node_gain,
    grid_bias,
    grid_gain,
    grid_v,
    edge_v,
    edge_in,
    edge_out,
    node_in,
    node_out,
    grid_in,
    grid_out,
    mesh_cot,
    grid_cot,
    grid_proj,
    recv_row,
    lent_row,
    send_col,
    recv_col,
    first_v,
    slope_v,
    unit_v,
    inv_v,
    wanted_v,
    dfirst_v,
    rows_a,
    rows_c,
    node_first,
    node_mesh_grad,
    grid_grad,
    grid_sum,
    load_sem,
    a_send,
    a_recv,
    c_send,
    c_recv,
    lend_send,
    lend_recv,
    *sum_refs,
):
    blocks, cap, width, mesh_rows, grid_rows = sizes
    lanes = 128
    fast = lax.axis_size("mesh")
    total = lax.axis_size("grid") * fast
    me = lax.axis_index("grid") * fast + lax.axis_index("mesh")
    core = lax.rem(me, 2)

    def at(shift):
        p = lax.rem(me + (shift + total), total)
        return (lax.div(p, fast), lax.rem(p, fast))

    twin = at(1 - 2 * core)

    def remote(src, dst, send_sem, recv_sem, device):
        return pltpu.make_async_remote_copy(
            src_ref=src,
            dst_ref=dst,
            send_sem=send_sem,
            recv_sem=recv_sem,
            device_id=device,
            device_id_type=pl.DeviceIdType.MESH,
        )

    wide = pl.ds(0, width)
    mid = pl.ds(width, width)
    last = pl.ds(2 * width, width)
    pairs = [
        (grid_hbm, grid_v),
        (edge_in_hbm.at[mid], edge_in.at[mid]),
        (edge_in_hbm.at[wide], edge_in.at[wide]),
        (edge_hbm.at[0], edge_v.at[pl.ds(0, blocks)]),
        (edge_in_hbm.at[last], edge_in.at[last]),
        (mesh_hbm, rows_a.at[4]),
        (edge_out_hbm, edge_out),
        (node_in_hbm, node_in),
        (node_out_hbm, node_out),
        (mesh_cot_hbm, mesh_cot),
        (grid_in_hbm, grid_in),
        (grid_out_hbm, grid_out),
        (grid_cot_hbm, grid_cot),
    ]
    small = [
        (count_hbm, count),
        (sender_hbm, sender),
        (receiver_hbm, receiver),
        (edge_bias_hbm, edge_bias),
        (edge_gain_hbm, edge_gain),
        (node_bias_hbm, node_bias),
        (node_gain_hbm, node_gain),
        (grid_bias_hbm, grid_bias),
        (grid_gain_hbm, grid_gain),
    ]
    few = [
        pltpu.make_async_copy(src, dst, load_sem.at[len(pairs) + i])
        for i, (src, dst) in enumerate(small)
    ]
    loads = [pltpu.make_async_copy(src, dst, load_sem.at[i]) for i, (src, dst) in enumerate(pairs)]
    barrier = pltpu.get_barrier_semaphore()
    partners = [at(2), at(-2), at(8), at(-8), twin]
    for partner in partners:
        pl.semaphore_signal(
            barrier, inc=1, device_id=partner, device_id_type=pl.DeviceIdType.MESH
        )

    def vector(ref):
        return ref[...].astype(F32).reshape(1, width)

    def part_rows(part):
        rows = mesh_rows // PARTS
        return pl.ds(pl.multiple_of(part * rows, rows), rows)

    far = 8 - 8 * core
    onward = 2 - 4 * core

    def spread_copy(i, part, spread):
        src, dst, device = [
            (4, 2, at(2)),
            (4, 6, at(-2)),
            (4, 3 + 2 * core, twin),
            (2 + 4 * (1 - core), far, at(-onward)),
            (2, 1 + 2 * core, twin),
            (6, 5 + 2 * core, twin),
            (far, 7 - 6 * core, twin),
        ][i]
        own = part_rows(part)
        return remote(
            spread.own.at[own] if i < 3 else spread.rows.at[src, own],
            spread.rows.at[dst, own],
            spread.send.at[i, part],
            spread.recv.at[dst, part],
            device,
        )

    def spread_arrived(slot, part, spread):
        own = spread.rows.at[slot, part_rows(part)]
        remote(own, own, spread.send.at[0, part], spread.recv.at[slot, part], twin).wait_recv()

    def spread_whole(slot, spread):
        for part in range(PARTS):
            spread_arrived(slot, part, spread)

    def spread_own(part, spread):
        for i in (0, 1, 2):
            spread_copy(i, part, spread).start()

    def spread_near(part, spread):
        spread_arrived(2, part, spread)
        spread_arrived(6, part, spread)
        for i in (3, 4, 5):
            spread_copy(i, part, spread).start()

    def spread_far(part, spread):
        spread_arrived(far, part, spread)
        spread_copy(6, part, spread).start()

    def spread_sent(spread):
        for part in range(PARTS):
            for i in range(7):
                spread_copy(i, part, spread).wait_send()

    def pair_copy(k, sums):
        slot = lax.div(k - 1 + 2 * core, 2)
        return remote(
            sums.part.at[k], sums.pair.at[slot], sums.pair_send.at[k], sums.pair_recv.at[slot], twin
        )

    def pair_arrived(slot, sums):
        own = sums.pair.at[slot]
        remote(own, own, sums.pair_send.at[1], sums.pair_recv.at[slot], twin).wait_recv()

    early = 2 + 4 * core
    late = 6 - 4 * core

    def early_copy(part, sums):
        own = part_rows(part)
        return remote(
            sums.part.at[early, own],
            sums.land.at[1 - core, own],
            sums.send.at[0, part],
            sums.land_recv.at[1 - core, part],
            at(-onward),
        )

    def late_copy(part, sums):
        own = part_rows(part)
        return remote(
            sums.part.at[late, own],
            sums.land.at[core, own],
            sums.send.at[1, part],
            sums.land_recv.at[core, part],
            at(onward),
        )

    def far_copy(part, sums):
        own = part_rows(part)
        return remote(
            sums.part.at[far, own],
            sums.cross.at[own],
            sums.send.at[2, part],
            sums.cross_recv.at[part],
            at(onward),
        )

    def join(k, own, sums, *more):
        value = sums.part[k, own].astype(F32) + sums.pair[lax.div(k, 2), own].astype(F32)
        for other in more:
            value = value + other.astype(F32)
        sums.part[k, own] = value.astype(BF16)

    def sum_early(sums):
        pair_arrived(lax.div(early, 2), sums)
        for part in range(PARTS):
            join(early, part_rows(part), sums)
            early_copy(part, sums).start()

    def sum_far(sums):
        pair_arrived(lax.div(far, 2), sums)
        for part in range(PARTS):
            join(far, part_rows(part), sums)
            far_copy(part, sums).start()

    def sum_late(sums):
        pair_arrived(lax.div(late, 2), sums)
        pair_arrived(2, sums)
        for part in range(PARTS):
            own = part_rows(part)
            far_copy(part, sums).wait_recv()
            join(late, own, sums, sums.cross[own])
            late_copy(part, sums).start()

    def summed(part, sums):
        own = part_rows(part)
        early_copy(part, sums).wait_recv()
        late_copy(part, sums).wait_recv()
        value = sums.part[4, own].astype(F32) + sums.pair[2, own].astype(F32)
        return (value + sums.land[0, own].astype(F32) + sums.land[1, own].astype(F32)).astype(BF16)

    def sum_sent(sums):
        for k in (1, 3, 5, 7):
            pair_copy(k, sums).wait_send()
        for part in range(PARTS):
            for copy in (early_copy, late_copy, far_copy):
                copy(part, sums).wait_send()

    spread_a = SimpleNamespace(own=mesh_hbm, rows=rows_a, send=a_send, recv=a_recv)
    spread_c = SimpleNamespace(own=rows_c.at[4], rows=rows_c, send=c_send, recv=c_recv)
    sum_b, sum_d = [
        SimpleNamespace(
            part=refs[0],
            pair=refs[1],
            land=refs[2],
            cross=refs[3],
            pair_send=refs[4],
            pair_recv=refs[5],
            send=refs[6],
            land_recv=refs[7],
            cross_recv=refs[8],
        )
        for refs in (sum_refs[:9], sum_refs[9:])
    ]

    def lend_copy(i):
        src, dst, shift = [
            (edge_v.at[0], edge_v.at[blocks], -8),
            (first_v.at[0], first_v.at[blocks], -8),
            (recv_row.at[pl.ds(0, blocks)], lent_row, -8),
            (wanted_v.at[blocks], wanted_v.at[0], 8),
            (dfirst_v.at[blocks], dfirst_v.at[0], 8),
        ][i]
        return remote(src, dst, lend_send.at[i], lend_recv.at[i], at(shift))

    last_z = lax.div(lax.axis_index("mesh"), 2) == lax.div(fast, 2) - 1

    def give_back(later):
        if not later:
            lend_copy(3).start()

        @pl.when(last_z == later)
        def _():
            lend_copy(4).start()

    def on_even(*steps):
        @pl.when(core == 0)
        def _():
            for step in steps:
                step()

    def pick(column, n):
        tiles = -(-n // lanes)
        ids = jnp.concatenate([column] * tiles, axis=1)[:, :n]
        return jnp.where(lax.broadcasted_iota(jnp.int32, (cap, n), 1) == ids, 1.0, 0.0).astype(BF16)

    def put(row, n, start=0):
        ids = lax.broadcasted_iota(jnp.int32, (n, cap), 0) + start
        return jnp.where(ids == row, 1.0, 0.0).astype(BF16)

    for load in few:
        load.start()
    pl.semaphore_wait(barrier, len(partners))
    for part in range(PARTS):
        spread_own(part, spread_a)
    for load in loads:
        load.start()

    for load in few:
        load.wait()

    slot_index = lax.broadcasted_iota(jnp.int32, (1, cap), 1)
    for k in range(blocks):
        recv_row[k : k + 1, :] = jnp.where(slot_index < count[0, k], receiver[0, k : k + 1, :], -1)
    on_even(lend_copy(2).start)
    for src, dst in ((sender[0], send_col), (recv_row[:blocks, :], recv_col)):
        turned = jnp.transpose(src)
        for k in range(blocks):
            dst[k] = jnp.broadcast_to(turned[:, k : k + 1], (cap, lanes))

    for load in loads[:4]:
        load.wait()
    on_even(lend_copy(0).start)
    grid_proj[...] = mm(grid_v[...], edge_in[mid, :]).astype(BF16)

    def first_step(k, _):
        first_v[k] = (
            mm(edge_v[k], edge_in[wide, :])
            + mm(pick(send_col[k], grid_rows), grid_proj[...])
            + vector(edge_bias)
        ).astype(BF16)

        @pl.when(jnp.logical_and(k == 0, core == 0))
        def _():
            lend_copy(1).start()

        return 0

    lax.fori_loop(0, blocks // 2, first_step, 0)
    for part in range(PARTS // 2):
        spread_near(part, spread_a)
    lax.fori_loop(blocks // 2, blocks, first_step, 0)
    for load in loads[4:7]:
        load.wait()

    def step_blocks(t, swap):
        lane = lax.rem(4 + t + t * t, 8)
        other = lax.rem(lane + 9 - 2 * core, 8)
        lane = lane + lax.div(t, 3) * far
        move = (lax.div(t, 3) * (1 - core) if swap else 0) * (other - lane)
        return lane + move, other - move

    def forward_block(k):
        joined = mm(pick(recv_col[k], mesh_rows), rows_a[k]).astype(BF16)
        u = first_v[k].astype(F32) + mm(joined, edge_in[last, :])
        hidden, slope = silu_pair(u)
        slope_v[k] = slope.astype(BF16)
        unit, inv = normed(mm(hidden.astype(BF16), edge_out[...]))
        unit_v[k] = unit.astype(BF16)
        inv_v[k] = jnp.broadcast_to(inv, (cap, lanes))
        message = (edge_v[k].astype(F32) + vector(edge_gain) * unit).astype(BF16)
        sum_b.part[k] = mm(put(recv_row[pl.ds(k, 1), :], mesh_rows), message).astype(BF16)

    def backward_block(k):
        wanted = mm(pick(recv_col[k], mesh_rows), rows_c[k])
        wanted_v[k] = wanted.astype(BF16)
        dv = normed_back(wanted * vector(edge_gain), unit_v[k].astype(F32), inv_v[k][:, :1])
        dhidden = mm_t(dv.astype(BF16), edge_out[...])
        dfirst = (dhidden * slope_v[k].astype(F32)).astype(BF16)
        dfirst_v[k] = dfirst
        sum_d.part[k] = mm(put(recv_row[pl.ds(k, 1), :], mesh_rows), dfirst).astype(BF16)

    def all_blocks(block_fn, spread, sums, after_own, before_lent, after_lent, swap):
        def step(t, _):
            first, second = step_blocks(t, swap)

            @pl.when(t == 1)
            def _():
                for part in range(PARTS // 2, PARTS):
                    spread_near(part, spread)

            @pl.when(t == 3)
            def _():
                sum_early(sums)
                for part in range(PARTS // 2, PARTS):
                    spread_far(part, spread)
                if swap:
                    on_even(functools.partial(spread_whole, 1, spread))
                else:
                    on_even(*before_lent)

            block_fn(first)

            @pl.when(t == 0)
            def _():
                for step in after_own:
                    step()

            @pl.when(t == 2)
            def _():
                for part in range(PARTS // 2):
                    spread_far(part, spread)

            @pl.when(t == 3)
            def _():
                if swap:
                    on_even(pair_copy(1, sums).start, *before_lent)
                else:
                    on_even(*after_lent)

            twin_second = jnp.logical_or(t < 3, core == 1) if swap else t >= 0

            @pl.when(twin_second)
            def _():
                spread_whole(second, spread)

            block_fn(second)

            @pl.when(twin_second)
            def _():
                pair_copy(second, sums).start()

            return 0

        lax.fori_loop(0, blocks // 2, step, 0)
        sum_far(sums)

    def lent_columns():
        recv_row[blocks : blocks + 1, :] = lent_row[0:1, :]
        turned = jnp.transpose(lent_row[...])
        recv_col[blocks] = jnp.broadcast_to(turned[:, 0:1], (cap, lanes))

    all_blocks(
        forward_block,
        spread_a,
        sum_b,
        [],
        [lend_copy(i).wait_recv for i in (0, 1, 2)] + [lent_columns],
        [],
        True,
    )

    def grid_step(i, _):
        rows = pl.ds(pl.multiple_of(i * cap, cap), cap)
        own = grid_v[rows, :]
        hidden, slope = silu_pair(mm(own, grid_in[...]) + vector(grid_bias))
        unit, inv = normed(mm(hidden.astype(BF16), grid_out[...]))
        grid_up[rows, :] = (own.astype(F32) + vector(grid_gain) * unit).astype(BF16)
        cot = grid_cot[rows, :].astype(F32)
        dv = normed_back(cot * vector(grid_gain), unit, inv)
        dfirst = (mm_t(dv.astype(BF16), grid_out[...]) * slope).astype(BF16)
        grid_grad[rows, :] = cot + mm_t(dfirst, grid_in[...])
        return 0


    def grid_part():
        for load in loads[10:13]:
            load.wait()
        lax.fori_loop(0, grid_rows // cap, grid_step, 0)

    for load in loads[7:10]:
        load.wait()
    node_first[...] = mm(rows_a[4], node_in[wide, :]) + vector(node_bias)
    grid_part()
    sum_late(sum_b)

    def node_step(part, _):
        own = part_rows(part)
        hidden, slope = silu_pair(node_first[own, :] + mm(summed(part, sum_b), node_in[mid, :]))
        unit, inv = normed(mm(hidden.astype(BF16), node_out[...]))
        cot = mesh_cot[own, :].astype(F32)
        dv = normed_back(cot * vector(node_gain), unit, inv)
        dfirst = (mm_t(dv.astype(BF16), node_out[...]) * slope).astype(BF16)
        rows_c[4, own] = mm_t(dfirst, node_in[mid, :]).astype(BF16)
        spread_own(part, spread_c)
        node_mesh_grad[own, :] = cot + mm_t(dfirst, node_in[wide, :])
        mesh_up[own, :] = (rows_a[4, own].astype(F32) + vector(node_gain) * unit).astype(BF16)
        return 0

    lax.fori_loop(0, PARTS, node_step, 0)

    all_blocks(
        backward_block,
        spread_c,
        sum_d,
        [functools.partial(spread_near, part, spread_c) for part in range(PARTS // 2)],
        [],
        [functools.partial(give_back, False)],
        False,
    )

    def edge_step(i, _):
        k = lax.rem(i + 1, blocks)
        grad_edge[0, k] = (
            wanted_v[k].astype(F32) + mm_t(dfirst_v[k], edge_in[wide, :])
        ).astype(BF16)
        return 0

    def grid_sum_step(i, _):
        start = pl.multiple_of(i * cap, cap)
        value = mm(put(sender[0, 1:2, :], cap, start), dfirst_v[1])
        for k in range(2, blocks):
            value = value + mm(put(sender[0, k : k + 1, :], cap, start), dfirst_v[k])
        grid_sum[pl.ds(start, cap), :] = value
        return 0

    def grid_last_step(i, _):
        start = pl.multiple_of(i * cap, cap)
        rows = pl.ds(start, cap)
        value = grid_sum[rows, :] + mm(put(sender[0, 0:1, :], cap, start), dfirst_v[0])
        grad_grid[rows, :] = (
            grid_grad[rows, :] + mm_t(value.astype(BF16), edge_in[mid, :])
        ).astype(BF16)
        return 0

    lax.fori_loop(0, blocks - 1, edge_step, 0)
    sum_late(sum_d)
    on_even(functools.partial(give_back, True))
    lax.fori_loop(0, grid_rows // cap, grid_sum_step, 0)
    on_even(lend_copy(3).wait_recv, lend_copy(4).wait_recv)
    lax.fori_loop(blocks - 1, blocks, edge_step, 0)
    lax.fori_loop(0, grid_rows // cap, grid_last_step, 0)

    for part in range(PARTS):
        own = part_rows(part)
        grad_mesh[own, :] = (
            node_mesh_grad[own, :] + mm_t(summed(part, sum_d), edge_in[last, :])
        ).astype(BF16)

    spread_sent(spread_a)
    sum_sent(sum_b)
    spread_sent(spread_c)
    sum_sent(sum_d)
    on_even(*[lend_copy(i).wait_send for i in range(5)])


def place_kernel(*refs):
    sources, targets, sems = refs[:5], refs[5:10], refs[10]
    copies = [pltpu.make_async_copy(sources[i], targets[i], sems.at[i]) for i in range(5)]
    for copy in copies:
        copy.start()
    for copy in copies:
        copy.wait()


def on_device(
    grid_latent,
    mesh_latent,
    edge_latent,
    edge_sender,
    edge_receiver,
    edge_count,
    edge_in_weight,
    edge_bias,
    edge_out_weight,
    edge_gain,
    node_in_weight,
    node_bias,
    node_out_weight,
    node_gain,
    grid_in_weight,
    grid_bias,
    grid_out_weight,
    grid_gain,
    mesh_cotangent,
    grid_cotangent,
):
    _, blocks, cap, width = edge_latent.shape
    mesh_rows, grid_rows = mesh_latent.shape[0], grid_latent.shape[0]
    anywhere = pl.BlockSpec(memory_space=pl.ANY)

    def buf(*shape, dtype=BF16):
        return pltpu.VMEM(shape, dtype)

    dma = pltpu.SemaphoreType.DMA
    more_slots = (blocks + 1, cap, width)
    block = (mesh_rows, width)
    scratch = [
        buf(*edge_sender.shape, dtype=jnp.int32),
        buf(*edge_receiver.shape, dtype=jnp.int32),
        pltpu.SMEM(edge_count.shape, jnp.int32),
        buf(width),
        buf(width),
        buf(width),
        buf(width),
        buf(width),
        buf(width),
        buf(grid_rows, width),
        buf(*more_slots),
        buf(3 * width, width),
        buf(width, width),
        buf(2 * width, width),
        buf(width, width),
        buf(width, width),
        buf(width, width),
        buf(mesh_rows, width),
        buf(grid_rows, width),
        buf(grid_rows, width),
        buf(2 * blocks, cap, dtype=jnp.int32),
        buf(blocks, cap, dtype=jnp.int32),
        buf(blocks, cap, 128, dtype=jnp.int32),
        buf(blocks + 1, cap, 128, dtype=jnp.int32),
        buf(*more_slots),
        buf(*more_slots),
        buf(*more_slots),
        buf(blocks + 1, cap, 128, dtype=F32),
        buf(*more_slots),
        buf(*more_slots),
        buf(blocks + 1, *block),
        buf(blocks + 1, *block),
        buf(*block, dtype=F32),
        buf(*block, dtype=F32),
        buf(grid_rows, width, dtype=F32),
        buf(grid_rows, width, dtype=F32),
        dma((22,)),
        dma((7, PARTS)),
        dma((blocks + 1, PARTS)),
        dma((7, PARTS)),
        dma((blocks + 1, PARTS)),
        dma((5,)),
        dma((5,)),
    ]
    sums = [
        buf(blocks + 1, *block),
        buf(blocks // 2 + 1, *block),
        buf(2, *block),
        buf(*block),
        dma((blocks,)),
        dma((blocks // 2 + 1,)),
        dma((3, PARTS)),
        dma((2, PARTS)),
        dma((PARTS,)),
    ]
    scratch = scratch + sums + sums
    outs = [
        jax.ShapeDtypeStruct(mesh_latent.shape, BF16),
        jax.ShapeDtypeStruct(grid_latent.shape, BF16),
        jax.ShapeDtypeStruct(grid_latent.shape, BF16),
        jax.ShapeDtypeStruct(mesh_latent.shape, BF16),
        jax.ShapeDtypeStruct(edge_latent.shape, BF16),
    ]
    results = pl.pallas_call(
        functools.partial(kernel, (blocks, cap, width, mesh_rows, grid_rows)),
        out_shape=[pltpu.VMEM(out.shape, out.dtype) for out in outs],
        in_specs=[anywhere] * 20,
        out_specs=[pl.BlockSpec(memory_space=pltpu.VMEM)] * 5,
        scratch_shapes=scratch,
        compiler_params=pltpu.CompilerParams(
            collective_id=0, has_side_effects=True, vmem_limit_bytes=52 * 2**20
        ),
        cost_estimate=pl.CostEstimate(
            flops=13_000_000_000, bytes_accessed=16_000_000, transcendentals=3_000_000
        ),
        name="encoder",
    )(
        grid_latent,
        mesh_latent,
        edge_latent,
        edge_sender,
        edge_receiver,
        edge_count,
        edge_in_weight,
        edge_out_weight,
        node_in_weight,
        node_out_weight,
        grid_in_weight,
        grid_out_weight,
        edge_bias,
        edge_gain,
        node_bias,
        node_gain,
        grid_bias,
        grid_gain,
        mesh_cotangent,
        grid_cotangent,
    )
    return pl.pallas_call(
        place_kernel,
        out_shape=outs,
        in_specs=[anywhere] * 5,
        out_specs=[anywhere] * 5,
        scratch_shapes=[dma((5,))],
        compiler_params=pltpu.CompilerParams(vmem_limit_bytes=16 * 2**20),
        name="place",
    )(*results)


def solution(mesh):
    rows = P(("grid", "mesh"), None)
    wide = P(("grid", "mesh"), None, None)
    slots = P(("grid", "mesh"), None, None, None)
    return jax.shard_map(
        on_device,
        mesh=mesh,
        in_specs=(rows, rows, slots, wide, wide, rows) + (P(),) * 12 + (rows, rows),
        out_specs=(rows, rows, rows, rows, slots),
        check_vma=False,
    )
```

```python
import functools
from types import SimpleNamespace

import jax
import jax.numpy as jnp
from jax import lax
from jax.experimental import pallas as pl
from jax.experimental.pallas import tpu as pltpu
from jax.sharding import PartitionSpec as P

F32 = jnp.float32
BF16 = jnp.bfloat16
PARTS = 2


def mm(a, b):
    return jnp.dot(a, b, preferred_element_type=F32)


def mm_t(a, b):
    return lax.dot_general(a, b, (((1,), (1,)), ((), ())), preferred_element_type=F32)


def silu_pair(u):
    gate = 0.5 + 0.5 * jnp.tanh(0.5 * u)
    value = u * gate
    return value, gate + value * (1.0 - gate)


def normed(v):
    centred = v - jnp.mean(v, axis=-1, keepdims=True)
    inv = lax.rsqrt(jnp.mean(centred * centred, axis=-1, keepdims=True) + 1e-05)
    return centred * inv, inv


def normed_back(dx, unit, inv):
    along = jnp.mean(dx * unit, axis=-1, keepdims=True)
    return inv * (dx - jnp.mean(dx, axis=-1, keepdims=True) - unit * along)


def kernel(
    sizes,
    grid_hbm,
    mesh_hbm,
    edge_hbm,
    sender_hbm,
    receiver_hbm,
    count_hbm,
    edge_in_hbm,
    edge_out_hbm,
    node_in_hbm,
    node_out_hbm,
    grid_in_hbm,
    grid_out_hbm,
    edge_bias_hbm,
    edge_gain_hbm,
    node_bias_hbm,
    node_gain_hbm,
    grid_bias_hbm,
    grid_gain_hbm,
    mesh_cot_hbm,
    grid_cot_hbm,
    mesh_up,
    grid_up,
    grad_grid,
    grad_mesh,
    grad_edge,
    sender,
    receiver,
    count,
    edge_bias,
    edge_gain,
    node_bias,
    node_gain,
    grid_bias,
    grid_gain,
    grid_v,
    edge_v,
    edge_in,
    edge_out,
    node_in,
    node_out,
    grid_in,
    grid_out,
    mesh_cot,
    grid_cot,
    grid_proj,
    recv_row,
    lent_row,
    send_col,
    recv_col,
    first_v,
    slope_v,
    unit_v,
    inv_v,
    wanted_v,
    dfirst_v,
    rows_a,
    rows_c,
    node_first,
    node_mesh_grad,
    grid_grad,
    grid_sum,
    load_sem,
    a_send,
    a_recv,
    c_send,
    c_recv,
    lend_send,
    lend_recv,
    *sum_refs,
):
    blocks, cap, width, mesh_rows, grid_rows = sizes
    lanes = 128
    fast = lax.axis_size("mesh")
    total = lax.axis_size("grid") * fast
    me = lax.axis_index("grid") * fast + lax.axis_index("mesh")
    core = lax.rem(me, 2)

    def at(shift):
        p = lax.rem(me + (shift + total), total)
        return (lax.div(p, fast), lax.rem(p, fast))

    twin = at(1 - 2 * core)

    def remote(src, dst, send_sem, recv_sem, device):
        return pltpu.make_async_remote_copy(
            src_ref=src,
            dst_ref=dst,
            send_sem=send_sem,
            recv_sem=recv_sem,
            device_id=device,
            device_id_type=pl.DeviceIdType.MESH,
        )

    wide = pl.ds(0, width)
    mid = pl.ds(width, width)
    last = pl.ds(2 * width, width)
    pairs = [
        (grid_hbm, grid_v),
        (edge_in_hbm.at[mid], edge_in.at[mid]),
        (edge_in_hbm.at[wide], edge_in.at[wide]),
        (edge_hbm.at[0], edge_v.at[pl.ds(0, blocks)]),
        (edge_in_hbm.at[last], edge_in.at[last]),
        (mesh_hbm, rows_a.at[4]),
        (edge_out_hbm, edge_out),
        (node_in_hbm, node_in),
        (node_out_hbm, node_out),
        (mesh_cot_hbm, mesh_cot),
        (grid_in_hbm, grid_in),
        (grid_out_hbm, grid_out),
        (grid_cot_hbm, grid_cot),
    ]
    small = [
        (count_hbm, count),
        (sender_hbm, sender),
        (receiver_hbm, receiver),
        (edge_bias_hbm, edge_bias),
        (edge_gain_hbm, edge_gain),
        (node_bias_hbm, node_bias),
        (node_gain_hbm, node_gain),
        (grid_bias_hbm, grid_bias),
        (grid_gain_hbm, grid_gain),
    ]
    few = [
        pltpu.make_async_copy(src, dst, load_sem.at[len(pairs) + i])
        for i, (src, dst) in enumerate(small)
    ]
    loads = [pltpu.make_async_copy(src, dst, load_sem.at[i]) for i, (src, dst) in enumerate(pairs)]
    barrier = pltpu.get_barrier_semaphore()
    partners = [at(2), at(-2), at(8), at(-8), twin]
    for partner in partners:
        pl.semaphore_signal(
            barrier, inc=1, device_id=partner, device_id_type=pl.DeviceIdType.MESH
        )

    def vector(ref):
        return ref[...].astype(F32).reshape(1, width)

    def part_rows(part):
        rows = mesh_rows // PARTS
        return pl.ds(pl.multiple_of(part * rows, rows), rows)

    far = 8 - 8 * core
    onward = 2 - 4 * core

    def spread_copy(i, part, spread):
        src, dst, device = [
            (4, 2, at(2)),
            (4, 6, at(-2)),
            (4, 3 + 2 * core, twin),
            (2 + 4 * (1 - core), far, at(-onward)),
            (2, 1 + 2 * core, twin),
            (6, 5 + 2 * core, twin),
            (far, 7 - 6 * core, twin),
        ][i]
        own = part_rows(part)
        return remote(
            spread.own.at[own] if i < 3 else spread.rows.at[src, own],
            spread.rows.at[dst, own],
            spread.send.at[i, part],
            spread.recv.at[dst, part],
            device,
        )

    def spread_arrived(slot, part, spread):
        own = spread.rows.at[slot, part_rows(part)]
        remote(own, own, spread.send.at[0, part], spread.recv.at[slot, part], twin).wait_recv()

    def spread_whole(slot, spread):
        for part in range(PARTS):
            spread_arrived(slot, part, spread)

    def spread_own(part, spread):
        for i in (0, 1, 2):
            spread_copy(i, part, spread).start()

    def spread_near(part, spread):
        spread_arrived(2, part, spread)
        spread_arrived(6, part, spread)
        for i in (3, 4, 5):
            spread_copy(i, part, spread).start()

    def spread_far(part, spread):
        spread_arrived(far, part, spread)
        spread_copy(6, part, spread).start()

    def spread_sent(spread):
        for part in range(PARTS):
            for i in range(7):
                spread_copy(i, part, spread).wait_send()

    def pair_copy(k, sums):
        slot = lax.div(k - 1 + 2 * core, 2)
        return remote(
            sums.part.at[k], sums.pair.at[slot], sums.pair_send.at[k], sums.pair_recv.at[slot], twin
        )

    def pair_arrived(slot, sums):
        own = sums.pair.at[slot]
        remote(own, own, sums.pair_send.at[1], sums.pair_recv.at[slot], twin).wait_recv()

    early = 2 + 4 * core
    late = 6 - 4 * core

    def early_copy(part, sums):
        own = part_rows(part)
        return remote(
            sums.part.at[early, own],
            sums.land.at[1 - core, own],
            sums.send.at[0, part],
            sums.land_recv.at[1 - core, part],
            at(-onward),
        )

    def late_copy(part, sums):
        own = part_rows(part)
        return remote(
            sums.part.at[late, own],
            sums.land.at[core, own],
            sums.send.at[1, part],
            sums.land_recv.at[core, part],
            at(onward),
        )

    def far_copy(part, sums):
        own = part_rows(part)
        return remote(
            sums.part.at[far, own],
            sums.cross.at[own],
            sums.send.at[2, part],
            sums.cross_recv.at[part],
            at(onward),
        )

    def join(k, own, sums, *more):
        value = sums.part[k, own].astype(F32) + sums.pair[lax.div(k, 2), own].astype(F32)
        for other in more:
            value = value + other.astype(F32)
        sums.part[k, own] = value.astype(BF16)

    def sum_early(sums):
        pair_arrived(lax.div(early, 2), sums)
        for part in range(PARTS):
            join(early, part_rows(part), sums)
            early_copy(part, sums).start()

    def sum_far(sums):
        pair_arrived(lax.div(far, 2), sums)
        for part in range(PARTS):
            join(far, part_rows(part), sums)
            far_copy(part, sums).start()

    def sum_late(sums):
        pair_arrived(lax.div(late, 2), sums)
        pair_arrived(2, sums)
        for part in range(PARTS):
            own = part_rows(part)
            far_copy(part, sums).wait_recv()
            join(late, own, sums, sums.cross[own])
            late_copy(part, sums).start()

    def summed(part, sums):
        own = part_rows(part)
        early_copy(part, sums).wait_recv()
        late_copy(part, sums).wait_recv()
        value = sums.part[4, own].astype(F32) + sums.pair[2, own].astype(F32)
        return (value + sums.land[0, own].astype(F32) + sums.land[1, own].astype(F32)).astype(BF16)

    def sum_sent(sums):
        for k in (1, 3, 5, 7):
            pair_copy(k, sums).wait_send()
        for part in range(PARTS):
            for copy in (early_copy, late_copy, far_copy):
                copy(part, sums).wait_send()

    spread_a = SimpleNamespace(own=mesh_hbm, rows=rows_a, send=a_send, recv=a_recv)
    spread_c = SimpleNamespace(own=rows_c.at[4], rows=rows_c, send=c_send, recv=c_recv)
    sum_b, sum_d = [
        SimpleNamespace(
            part=refs[0],
            pair=refs[1],
            land=refs[2],
            cross=refs[3],
            pair_send=refs[4],
            pair_recv=refs[5],
            send=refs[6],
            land_recv=refs[7],
            cross_recv=refs[8],
        )
        for refs in (sum_refs[:9], sum_refs[9:])
    ]

    def lend_copy(i):
        src, dst, shift = [
            (edge_v.at[0], edge_v.at[blocks], -8),
            (first_v.at[0], first_v.at[blocks], -8),
            (recv_row.at[pl.ds(0, blocks)], lent_row, -8),
            (wanted_v.at[blocks], wanted_v.at[0], 8),
            (dfirst_v.at[blocks], dfirst_v.at[0], 8),
        ][i]
        return remote(src, dst, lend_send.at[i], lend_recv.at[i], at(shift))

    last_z = lax.div(lax.axis_index("mesh"), 2) == lax.div(fast, 2) - 1

    def give_back(later):
        if not later:
            lend_copy(3).start()

        @pl.when(last_z == later)
        def _():
            lend_copy(4).start()

    def on_even(*steps):
        @pl.when(core == 0)
        def _():
            for step in steps:
                step()

    def pick(column, n):
        tiles = -(-n // lanes)
        ids = jnp.concatenate([column] * tiles, axis=1)[:, :n]
        return jnp.where(lax.broadcasted_iota(jnp.int32, (cap, n), 1) == ids, 1.0, 0.0).astype(BF16)

    def put(row, n, start=0):
        ids = lax.broadcasted_iota(jnp.int32, (n, cap), 0) + start
        return jnp.where(ids == row, 1.0, 0.0).astype(BF16)

    for load in few:
        load.start()
    pl.semaphore_wait(barrier, len(partners))
    for part in range(PARTS):
        spread_own(part, spread_a)
    for load in loads:
        load.start()

    for load in few:
        load.wait()

    slot_index = lax.broadcasted_iota(jnp.int32, (1, cap), 1)
    for k in range(blocks):
        recv_row[k : k + 1, :] = jnp.where(slot_index < count[0, k], receiver[0, k : k + 1, :], -1)
    on_even(lend_copy(2).start)
    for src, dst in ((sender[0], send_col), (recv_row[:blocks, :], recv_col)):
        turned = jnp.transpose(src)
        for k in range(blocks):
            dst[k] = jnp.broadcast_to(turned[:, k : k + 1], (cap, lanes))

    for load in loads[:4]:
        load.wait()
    on_even(lend_copy(0).start)
    grid_proj[...] = mm(grid_v[...], edge_in[mid, :]).astype(BF16)

    def first_step(k, _):
        first_v[k] = (
            mm(edge_v[k], edge_in[wide, :])
            + mm(pick(send_col[k], grid_rows), grid_proj[...])
            + vector(edge_bias)
        ).astype(BF16)

        @pl.when(jnp.logical_and(k == 0, core == 0))
        def _():
            lend_copy(1).start()

        return 0

    lax.fori_loop(0, blocks // 2, first_step, 0)
    for part in range(PARTS // 2):
        spread_near(part, spread_a)
    lax.fori_loop(blocks // 2, blocks, first_step, 0)
    for load in loads[4:7]:
        load.wait()

    def step_blocks(t, swap):
        turn = lax.rem(4 + t + t * t, 8)
        lane = turn + (1 - core) * (8 - 2 * turn)
        other = (1 - core) * (turn + 1) + core * (7 - turn)
        move = (lax.div(t, 3) * (1 - core) if swap else 0) * (other - lane)
        return lane + move, other - move

    def forward_block(k):
        joined = mm(pick(recv_col[k], mesh_rows), rows_a[k]).astype(BF16)
        u = first_v[k].astype(F32) + mm(joined, edge_in[last, :])
        hidden, slope = silu_pair(u)
        slope_v[k] = slope.astype(BF16)
        unit, inv = normed(mm(hidden.astype(BF16), edge_out[...]))
        unit_v[k] = unit.astype(BF16)
        inv_v[k] = jnp.broadcast_to(inv, (cap, lanes))
        message = (edge_v[k].astype(F32) + vector(edge_gain) * unit).astype(BF16)
        sum_b.part[k] = mm(put(recv_row[pl.ds(k, 1), :], mesh_rows), message).astype(BF16)

    def backward_block(k):
        wanted = mm(pick(recv_col[k], mesh_rows), rows_c[k])
        wanted_v[k] = wanted.astype(BF16)
        dv = normed_back(wanted * vector(edge_gain), unit_v[k].astype(F32), inv_v[k][:, :1])
        dhidden = mm_t(dv.astype(BF16), edge_out[...])
        dfirst = (dhidden * slope_v[k].astype(F32)).astype(BF16)
        dfirst_v[k] = dfirst
        sum_d.part[k] = mm(put(recv_row[pl.ds(k, 1), :], mesh_rows), dfirst).astype(BF16)

    def all_blocks(block_fn, spread, sums, after_own, before_lent, after_lent, swap):
        def step(t, _):
            first, second = step_blocks(t, swap)

            @pl.when(t == 1)
            def _():
                for part in range(PARTS // 2, PARTS):
                    spread_near(part, spread)

            @pl.when(t == 3)
            def _():
                for part in range(PARTS // 2, PARTS):
                    spread_far(part, spread)
                if swap:
                    on_even(functools.partial(spread_whole, 1, spread))
                else:
                    on_even(*before_lent)

            block_fn(first)

            @pl.when(t == 0)
            def _():
                for step in after_own:
                    step()

            @pl.when(t == 2)
            def _():
                sum_early(sums)
                for part in range(PARTS // 2):
                    spread_far(part, spread)

            @pl.when(t == 3)
            def _():
                if swap:
                    on_even(pair_copy(1, sums).start, *before_lent)
                else:
                    on_even(*after_lent)

            twin_second = jnp.logical_or(t < 3, core == 1) if swap else t >= 0

            @pl.when(twin_second)
            def _():
                spread_whole(second, spread)

            block_fn(second)

            @pl.when(twin_second)
            def _():
                pair_copy(second, sums).start()

            return 0

        lax.fori_loop(0, blocks // 2, step, 0)
        sum_far(sums)

    def lent_columns():
        recv_row[blocks : blocks + 1, :] = lent_row[0:1, :]
        turned = jnp.transpose(lent_row[...])
        recv_col[blocks] = jnp.broadcast_to(turned[:, 0:1], (cap, lanes))

    all_blocks(
        forward_block,
        spread_a,
        sum_b,
        [],
        [lend_copy(i).wait_recv for i in (0, 1, 2)] + [lent_columns],
        [],
        True,
    )

    def grid_step(i, _):
        rows = pl.ds(pl.multiple_of(i * cap, cap), cap)
        own = grid_v[rows, :]
        hidden, slope = silu_pair(mm(own, grid_in[...]) + vector(grid_bias))
        unit, inv = normed(mm(hidden.astype(BF16), grid_out[...]))
        grid_up[rows, :] = (own.astype(F32) + vector(grid_gain) * unit).astype(BF16)
        cot = grid_cot[rows, :].astype(F32)
        dv = normed_back(cot * vector(grid_gain), unit, inv)
        dfirst = (mm_t(dv.astype(BF16), grid_out[...]) * slope).astype(BF16)
        grid_grad[rows, :] = cot + mm_t(dfirst, grid_in[...])
        return 0


    def grid_part():
        for load in loads[10:13]:
            load.wait()
        lax.fori_loop(0, grid_rows // cap, grid_step, 0)

    for load in loads[7:10]:
        load.wait()
    node_first[...] = mm(rows_a[4], node_in[wide, :]) + vector(node_bias)
    grid_part()
    sum_late(sum_b)

    def node_step(part, _):
        own = part_rows(part)
        hidden, slope = silu_pair(node_first[own, :] + mm(summed(part, sum_b), node_in[mid, :]))
        unit, inv = normed(mm(hidden.astype(BF16), node_out[...]))
        cot = mesh_cot[own, :].astype(F32)
        dv = normed_back(cot * vector(node_gain), unit, inv)
        dfirst = (mm_t(dv.astype(BF16), node_out[...]) * slope).astype(BF16)
        rows_c[4, own] = mm_t(dfirst, node_in[mid, :]).astype(BF16)
        spread_own(part, spread_c)
        node_mesh_grad[own, :] = cot + mm_t(dfirst, node_in[wide, :])
        mesh_up[own, :] = (rows_a[4, own].astype(F32) + vector(node_gain) * unit).astype(BF16)
        return 0

    lax.fori_loop(0, PARTS, node_step, 0)

    all_blocks(
        backward_block,
        spread_c,
        sum_d,
        [functools.partial(spread_near, part, spread_c) for part in range(PARTS // 2)],
        [],
        [functools.partial(give_back, False)],
        False,
    )

    def edge_step(i, _):
        k = lax.rem(i + 1, blocks)
        grad_edge[0, k] = (
            wanted_v[k].astype(F32) + mm_t(dfirst_v[k], edge_in[wide, :])
        ).astype(BF16)
        return 0

    def grid_sum_step(i, _):
        start = pl.multiple_of(i * cap, cap)
        value = mm(put(sender[0, 1:2, :], cap, start), dfirst_v[1])
        for k in range(2, blocks):
            value = value + mm(put(sender[0, k : k + 1, :], cap, start), dfirst_v[k])
        grid_sum[pl.ds(start, cap), :] = value
        return 0

    def grid_last_step(i, _):
        start = pl.multiple_of(i * cap, cap)
        rows = pl.ds(start, cap)
        value = grid_sum[rows, :] + mm(put(sender[0, 0:1, :], cap, start), dfirst_v[0])
        grad_grid[rows, :] = (
            grid_grad[rows, :] + mm_t(value.astype(BF16), edge_in[mid, :])
        ).astype(BF16)
        return 0

    lax.fori_loop(0, blocks - 1, edge_step, 0)
    sum_late(sum_d)
    on_even(functools.partial(give_back, True))
    lax.fori_loop(0, grid_rows // cap, grid_sum_step, 0)
    on_even(lend_copy(3).wait_recv, lend_copy(4).wait_recv)
    lax.fori_loop(blocks - 1, blocks, edge_step, 0)
    lax.fori_loop(0, grid_rows // cap, grid_last_step, 0)

    for part in range(PARTS):
        own = part_rows(part)
        grad_mesh[own, :] = (
            node_mesh_grad[own, :] + mm_t(summed(part, sum_d), edge_in[last, :])
        ).astype(BF16)

    spread_sent(spread_a)
    sum_sent(sum_b)
    spread_sent(spread_c)
    sum_sent(sum_d)
    on_even(*[lend_copy(i).wait_send for i in range(5)])


def place_kernel(*refs):
    sources, targets, sems = refs[:5], refs[5:10], refs[10]
    copies = [pltpu.make_async_copy(sources[i], targets[i], sems.at[i]) for i in range(5)]
    for copy in copies:
        copy.start()
    for copy in copies:
        copy.wait()


def on_device(
    grid_latent,
    mesh_latent,
    edge_latent,
    edge_sender,
    edge_receiver,
    edge_count,
    edge_in_weight,
    edge_bias,
    edge_out_weight,
    edge_gain,
    node_in_weight,
    node_bias,
    node_out_weight,
    node_gain,
    grid_in_weight,
    grid_bias,
    grid_out_weight,
    grid_gain,
    mesh_cotangent,
    grid_cotangent,
):
    _, blocks, cap, width = edge_latent.shape
    mesh_rows, grid_rows = mesh_latent.shape[0], grid_latent.shape[0]
    anywhere = pl.BlockSpec(memory_space=pl.ANY)

    def buf(*shape, dtype=BF16):
        return pltpu.VMEM(shape, dtype)

    dma = pltpu.SemaphoreType.DMA
    more_slots = (blocks + 1, cap, width)
    block = (mesh_rows, width)
    scratch = [
        buf(*edge_sender.shape, dtype=jnp.int32),
        buf(*edge_receiver.shape, dtype=jnp.int32),
        pltpu.SMEM(edge_count.shape, jnp.int32),
        buf(width),
        buf(width),
        buf(width),
        buf(width),
        buf(width),
        buf(width),
        buf(grid_rows, width),
        buf(*more_slots),
        buf(3 * width, width),
        buf(width, width),
        buf(2 * width, width),
        buf(width, width),
        buf(width, width),
        buf(width, width),
        buf(mesh_rows, width),
        buf(grid_rows, width),
        buf(grid_rows, width),
        buf(2 * blocks, cap, dtype=jnp.int32),
        buf(blocks, cap, dtype=jnp.int32),
        buf(blocks, cap, 128, dtype=jnp.int32),
        buf(blocks + 1, cap, 128, dtype=jnp.int32),
        buf(*more_slots),
        buf(*more_slots),
        buf(*more_slots),
        buf(blocks + 1, cap, 128, dtype=F32),
        buf(*more_slots),
        buf(*more_slots),
        buf(blocks + 1, *block),
        buf(blocks + 1, *block),
        buf(*block, dtype=F32),
        buf(*block, dtype=F32),
        buf(grid_rows, width, dtype=F32),
        buf(grid_rows, width, dtype=F32),
        dma((22,)),
        dma((7, PARTS)),
        dma((blocks + 1, PARTS)),
        dma((7, PARTS)),
        dma((blocks + 1, PARTS)),
        dma((5,)),
        dma((5,)),
    ]
    sums = [
        buf(blocks + 1, *block),
        buf(blocks // 2 + 1, *block),
        buf(2, *block),
        buf(*block),
        dma((blocks,)),
        dma((blocks // 2 + 1,)),
        dma((3, PARTS)),
        dma((2, PARTS)),
        dma((PARTS,)),
    ]
    scratch = scratch + sums + sums
    outs = [
        jax.ShapeDtypeStruct(mesh_latent.shape, BF16),
        jax.ShapeDtypeStruct(grid_latent.shape, BF16),
        jax.ShapeDtypeStruct(grid_latent.shape, BF16),
        jax.ShapeDtypeStruct(mesh_latent.shape, BF16),
        jax.ShapeDtypeStruct(edge_latent.shape, BF16),
    ]
    results = pl.pallas_call(
        functools.partial(kernel, (blocks, cap, width, mesh_rows, grid_rows)),
        out_shape=[pltpu.VMEM(out.shape, out.dtype) for out in outs],
        in_specs=[anywhere] * 20,
        out_specs=[pl.BlockSpec(memory_space=pltpu.VMEM)] * 5,
        scratch_shapes=scratch,
        compiler_params=pltpu.CompilerParams(
            collective_id=0, has_side_effects=True, vmem_limit_bytes=52 * 2**20
        ),
        cost_estimate=pl.CostEstimate(
            flops=13_000_000_000, bytes_accessed=16_000_000, transcendentals=3_000_000
        ),
        name="encoder",
    )(
        grid_latent,
        mesh_latent,
        edge_latent,
        edge_sender,
        edge_receiver,
        edge_count,
        edge_in_weight,
        edge_out_weight,
        node_in_weight,
        node_out_weight,
        grid_in_weight,
        grid_out_weight,
        edge_bias,
        edge_gain,
        node_bias,
        node_gain,
        grid_bias,
        grid_gain,
        mesh_cotangent,
        grid_cotangent,
    )
    return pl.pallas_call(
        place_kernel,
        out_shape=outs,
        in_specs=[anywhere] * 5,
        out_specs=[anywhere] * 5,
        scratch_shapes=[dma((5,))],
        compiler_params=pltpu.CompilerParams(vmem_limit_bytes=16 * 2**20),
        name="place",
    )(*results)


def solution(mesh):
    rows = P(("grid", "mesh"), None)
    wide = P(("grid", "mesh"), None, None)
    slots = P(("grid", "mesh"), None, None, None)
    return jax.shard_map(
        on_device,
        mesh=mesh,
        in_specs=(rows, rows, slots, wide, wide, rows) + (P(),) * 12 + (rows, rows),
        out_specs=(rows, rows, rows, rows, slots),
        check_vma=False,
    )
```
